32 devices in a mesh: blk: 4 (over y, x), seq: 8 (over z, core).
Axes of the slice: x: 2, y: 2, z: 4, core: 2. Of those that a mesh axis runs over, the one named last changes fastest.
Arguments:
- tokens: bfloat16 [4, 2048, 1024], P('blk', 'seq'), may hold values from -128 to 128
- expert_ids: int32 [4, 2048, 1], P('blk', 'seq'), may hold values from 0 to 7; in each aligned block of 256 rows (0 to 255, 256 to 511, ..., all dimensions but the last counted through in order) at most 64 rows name the same one
- expert_capacity: int32 [8], replicated, may hold values from 32 to 64, as said below
- kernel_weight: bfloat16 [1024, 496], replicated, may hold values from -1 to 1
- norm_gain: bfloat16 [1024], replicated, may hold values from 0.25 to 1.75
- router: bfloat16 [1024, 8], replicated, may hold values from -0.1875 to 0.1875
- expert_gate: bfloat16 [8, 1024, 2048], P('seq', None, 'blk'), may hold values from -0.1875 to 0.1875
- expert_up: bfloat16 [8, 1024, 2048], P('seq', None, 'blk'), may hold values from -0.1875 to 0.1875
- expert_down: bfloat16 [8, 1024, 2048], P('seq', None, 'blk'), may hold values from -0.125 to 0.125
Outputs:
- result: bfloat16 [4, 2048, 1024], P('blk', 'seq')
The draws below stay inside these ranges and needn't reach their ends.
Inputs may be any that keep to these rules, and one draw needn't show every extreme that they name: `expert_ids`: in each aligned block of 256 positions (the positions of one device) no expert is named more than 64 times, a bound that some block reaches. `expert_capacity`: some expert has capacity exactly 64.
All inputs are finite; a program needn't handle non-finite values.
Results may differ from the reference program's by a relative error of at most 0.004.
Values may be sent and summed in bfloat16 or wider, within the bound.
No kernel may reach another device: no remote copies, remote signals or barrier semaphores. Data moves between devices by JAX's collectives and lax.ppermute only.
A program may use at most 128 MiB of HBM per device.

```python
import math
import jax
import jax.numpy as jnp
import numpy as np
from jax import lax

D = 1024
HEADS = 16
TAPS = 31
FF = 2048
TOK_DEV = 256
HEAD_DIM = 64
HALF = 15
SEQS = 4
LENGTH = 2048
EXPERTS = 8
CAP = 64
N_SEQ = 8


def kernel_base(key):
    values = jax.random.normal(jax.random.fold_in(key, 7), (D, HEADS * TAPS), jnp.float32)
    return jnp.clip(values, -5.0, 5.0) / math.sqrt(D)


def draw_kernel_weight(key, part):
    return kernel_base(key).astype(jnp.bfloat16)


def draw_expert_capacity(key, part):
    lower = max(1, CAP // 2)
    levels = jax.random.randint(jax.random.fold_in(key, 21), (EXPERTS,), lower, CAP + 1)
    which = jax.random.randint(jax.random.fold_in(key, 22), (), 0, EXPERTS)
    return jnp.where(jnp.arange(EXPERTS) == which, CAP, levels).astype(jnp.int32)


def draw_tokens(key, part):
    total = SEQS * LENGTH
    rows = jnp.clip(jax.random.normal(jax.random.fold_in(key, 17), (total, D), jnp.float32), -6.0, 6.0)
    return rows.reshape(SEQS, LENGTH, D).astype(jnp.bfloat16)


def shard_levels(key, shape, cuts, least, largest):
    loudness = 1.0
    for position, blocks in cuts:
        steps = jax.random.uniform(jax.random.fold_in(jax.random.fold_in(key, 6), position), (blocks,), jnp.float32, least / len(cuts), largest / len(cuts))
        loudness = loudness * jnp.repeat(jnp.exp(steps), shape[position] // blocks).reshape((-1,) + (1,) * (len(shape) - 1 - position))
    return loudness


def shared_out(own_key, own, number, rows, amount, top, most, slope):
    ranking = jax.random.permutation(own_key, amount)
    packed, usual = shares(amount, rows * top, most, slope, True), shares(amount, rows * top, most, slope, False)
    places = jnp.arange(amount)

    def named(tallies, offset_by):
        used = int((tallies > 0).sum())
        fixed = max(1, used // 4)
        moved = fixed + (places - fixed + offset_by * (used - fixed)) % max(1, amount - fixed)
        return jnp.zeros((amount,), jnp.int32).at[ranking[jnp.where(places < fixed, places, moved)]].set(jnp.asarray(tallies, jnp.int32))

    tallies = jnp.where(number % 4 == 0, named(packed, number // 4), named(usual, number - number // 4 - 1))
    mixed = jax.random.permutation(jax.random.fold_in(own, 3), amount)
    giver, sink = mixed[0:amount // 2 * 2:2], mixed[1:amount // 2 * 2:2]
    slack = jnp.minimum(tallies[giver] - 1, most - tallies[sink]) // 2
    slack = jnp.where((giver == ranking[0]) | (sink == ranking[0]) | (tallies[sink] == 0), 0, jnp.maximum(slack, 0))
    moved = jax.random.randint(jax.random.fold_in(own, 4), (amount // 2,), 0, 1 << 20) % (slack + 1)
    tallies = tallies.at[giver].add(-moved).at[sink].add(moved)
    items = jnp.searchsorted(jnp.cumsum(tallies), jnp.arange(rows * top), side="right").astype(jnp.int32)
    listing = items.reshape(top, rows).T
    listing = listing[jax.random.permutation(jax.random.fold_in(own, 1), rows)]
    offset_by = jax.random.randint(jax.random.fold_in(own, 2), (rows, 1), 0, top)
    return jnp.take_along_axis(listing, (jnp.arange(top)[None, :] + offset_by) % top, axis=1)


def shares(amount, total, bound, lean, full):
    loads = [(1 << 20) // math.isqrt(rank ** lean) + 1 for rank in range(1, amount + 1)]
    largest = bound if full else min(bound, max(-(-total // amount), total * loads[0] // sum(loads)))
    least = 1 if total - largest >= amount - 1 else 0
    holding, spare = [largest] + [least] * (amount - 1), total - largest - least * (amount - 1)
    while spare > 0:
        candidates = [i for i in range(1, amount) if holding[i] < largest] or [i for i in range(1, amount) if holding[i] < bound]
        whole, remaining = sum([loads[i] for i in candidates]), spare
        for i in candidates:
            extra = min(bound - holding[i], max(1, remaining * loads[i] // whole), spare)
            holding[i] = holding[i] + extra
            spare = spare - extra
    return np.array(holding)


def noise(key, extent, deviation, bound, cuts=(), held_as=jnp.bfloat16):
    level = shard_levels(key, extent, cuts, -0.22, 0.18) if cuts else 1.0
    values = jax.random.normal(key, extent, jnp.float32) * deviation * level
    return jnp.minimum(jnp.maximum(values, -bound), bound).astype(held_as)


def setup_inputs(seed: int = 0) -> dict:
    key_of = jax.random.split(jax.random.key(seed), 10)
    tokens = draw_tokens(jax.random.fold_in(key_of[9], 71), 0)
    expert_ids_keys = jax.random.split(jax.random.fold_in(key_of[1], 1), SEQS * LENGTH // TOK_DEV)
    expert_ids_turns = jax.random.permutation(jax.random.fold_in(key_of[1], 3), SEQS * LENGTH // TOK_DEV)
    expert_ids = jax.vmap(lambda own, number: shared_out(jax.random.fold_in(key_of[1], 2), own, number, TOK_DEV, EXPERTS, 1, CAP, 1))(expert_ids_keys, expert_ids_turns).reshape((SEQS, LENGTH, 1))
    expert_capacity = draw_expert_capacity(jax.random.fold_in(key_of[9], 71), 0)
    kernel_weight = draw_kernel_weight(jax.random.fold_in(key_of[9], 71), 0)
    norm_gain = jnp.clip(1.0 + 0.15 * jax.random.normal(key_of[4], (D,), jnp.float32), 0.25, 1.75).astype(jnp.bfloat16)
    router = noise(key_of[5], (D, EXPERTS), D ** -0.5, 0.1875)
    expert_gate = noise(key_of[6], (EXPERTS, D, FF), D ** -0.5, 0.1875, ((0, 8), (2, 4)))
    expert_up = noise(key_of[7], (EXPERTS, D, FF), D ** -0.5, 0.1875, ((0, 8), (2, 4)))
    expert_down = noise(key_of[8], (EXPERTS, D, FF), FF ** -0.5, 0.125, ((0, 8), (2, 4)))
    return dict(tokens=tokens, expert_ids=expert_ids, expert_capacity=expert_capacity, kernel_weight=kernel_weight, norm_gain=norm_gain, router=router, expert_gate=expert_gate, expert_up=expert_up, expert_down=expert_down)


EPS = 1e-06

def reference(tokens, expert_ids, expert_capacity, kernel_weight, norm_gain, router, expert_gate, expert_up, expert_down):
    flat = tokens.reshape(-1, D)
    logits = jnp.dot(flat, kernel_weight, preferred_element_type=jnp.float32).reshape(SEQS, LENGTH, HEADS, TAPS)
    probs = jax.nn.softmax(logits, axis=-1).astype(jnp.bfloat16)
    padded = jnp.pad(tokens, ((0, 0), (HALF, HALF), (0, 0)))
    mixed = tokens.astype(jnp.float32)
    for k in range(TAPS):
        weight = jnp.repeat(probs[:, :, :, k].astype(jnp.float32), HEAD_DIM, axis=2)
        mixed = mixed + weight * padded[:, k:k + LENGTH].astype(jnp.float32)
    scale = lax.rsqrt(lax.optimization_barrier(jnp.mean(mixed * mixed, axis=-1, keepdims=True)) + EPS)
    normed = (mixed * scale * norm_gain.astype(jnp.float32)).astype(jnp.bfloat16)
    blocks = SEQS * N_SEQ
    ids = expert_ids.reshape(blocks, TOK_DEV).astype(jnp.int32)
    onehot = (ids[:, :, None] == jnp.arange(EXPERTS, dtype=jnp.int32)[None, None, :]).astype(jnp.int32)
    rank = lax.optimization_barrier(jnp.sum((jnp.cumsum(onehot, axis=1) - 1) * onehot, axis=-1)).astype(jnp.int32)
    limit = expert_capacity[ids]
    kept = rank < limit
    gate_all = jnp.dot(normed.reshape(-1, D), router, preferred_element_type=jnp.float32)
    chosen = jnp.take_along_axis(gate_all, ids.reshape(-1, 1), axis=1).reshape(blocks, TOK_DEV)
    gate = jax.nn.sigmoid(chosen)
    slot = jnp.where(kept, ids * CAP + rank, EXPERTS * CAP).astype(jnp.int32)
    block_index = jnp.broadcast_to(jnp.arange(blocks, dtype=jnp.int32)[:, None], (blocks, TOK_DEV))
    normed_blocks = normed.reshape(blocks, TOK_DEV, D)
    buffer = jnp.zeros((blocks, EXPERTS * CAP + 1, D), jnp.bfloat16).at[block_index, slot].set(normed_blocks)
    buffer = buffer[:, :EXPERTS * CAP].reshape(blocks, EXPERTS, CAP, D)

    def expert_step(index):
        rows = buffer[:, index].reshape(-1, D)
        gated = jnp.dot(rows, expert_gate[index], preferred_element_type=jnp.float32)
        lifted = jnp.dot(rows, expert_up[index], preferred_element_type=jnp.float32)
        act = (jax.nn.silu(gated) * lifted).astype(jnp.bfloat16)
        output = lax.dot_general(act, expert_down[index], (((1,), (1,)), ((), ())), preferred_element_type=jnp.float32)
        return output.astype(jnp.bfloat16).reshape(blocks, CAP, D)
    outputs = lax.map(expert_step, jnp.arange(EXPERTS, dtype=jnp.int32))
    token_out = outputs[ids, block_index, jnp.minimum(rank, CAP - 1)].astype(jnp.float32)
    token_out = jnp.where(kept[:, :, None], token_out, jnp.float32(0.0))
    result = mixed.reshape(blocks, TOK_DEV, D) + gate[:, :, None] * token_out
    return result.astype(jnp.bfloat16).reshape(SEQS, LENGTH, D)
```

```python
import functools

import jax
import jax.numpy as jnp
from jax import lax
from jax.experimental import pallas as pl
from jax.experimental.pallas import tpu as pltpu
from jax.sharding import PartitionSpec as P

HEADS = 16
TAPS = 31
LANES = 32
HALO = 16
FRONT = 96
BLOCK = 128
EPS = 1e-06

VMEM = pl.BlockSpec(memory_space=pltpu.VMEM)
F32 = jnp.float32
BF16 = jnp.bfloat16


def iota(shape, dim):
    return lax.broadcasted_iota(jnp.int32, shape, dim)


def probs_kernel(tokens_ref, weight_ref, probs_ref):
    count = tokens_ref.shape[0]
    columns = weight_ref.shape[1]
    row = iota((columns, HEADS * LANES), 0)
    column = iota((columns, HEADS * LANES), 1)
    tap = column % LANES
    spread = jnp.where((column // LANES * TAPS + tap == row) & (tap < TAPS), 1.0, 0.0).astype(BF16)
    weight = jnp.dot(weight_ref[...], spread, preferred_element_type=F32).astype(BF16)
    logits = jnp.dot(tokens_ref[...], weight, preferred_element_type=F32)
    logits = logits.T.reshape(HEADS, LANES, count)
    used = iota(logits.shape, 1) < TAPS
    logits = jnp.where(used, logits, -3e38)
    top = jnp.max(logits, axis=1, keepdims=True)
    powers = jnp.exp(logits - top)
    probs = powers / jnp.sum(powers, axis=1, keepdims=True)
    probs_ref[...] = probs.reshape(HEADS * LANES, count).T.astype(BF16)


def slots_of(onehot, before, capacity, depth, axis):
    kept = jnp.sum(onehot * (before < capacity).astype(F32), axis=axis, keepdims=True) > 0.5
    expert = iota(onehot.shape, axis).astype(F32)
    slot = jnp.sum(onehot * (expert * depth + before), axis=axis, keepdims=True)
    return jnp.where(kept, slot, -1.0).astype(jnp.int32)


def mix_kernel(
    depth,
    tokens_ref,
    low_ref,
    high_ref,
    probs_ref,
    ids_row_ref,
    ids_ref,
    capacity_ref,
    capacity_row_ref,
    gain_ref,
    router_ref,
    mixed_ref,
    packed_ref,
    gate_ref,
    slot_ref,
    padded_ref,
    normed_ref,
):
    count, width = tokens_ref.shape
    experts = capacity_ref.shape[0]
    padded_ref[pl.ds(0, FRONT), :] = jnp.zeros((FRONT, width), BF16)
    padded_ref[pl.ds(FRONT, HALO), :] = low_ref[...]
    padded_ref[pl.ds(FRONT + HALO, count), :] = tokens_ref[...]
    padded_ref[pl.ds(FRONT + HALO + count, HALO), :] = high_ref[...]
    after = FRONT + 2 * HALO + count
    padded_ref[pl.ds(after, padded_ref.shape[0] - after), :] = jnp.zeros(
        (padded_ref.shape[0] - after, width), BF16
    )
    offset = iota((BLOCK, 2 * BLOCK), 1) - iota((BLOCK, 2 * BLOCK), 0) - 1
    squares = []
    for block in range(count // BLOCK):
        rows = pl.ds(block * BLOCK, BLOCK)
        square = jnp.zeros((BLOCK, 128), F32)
        for group in range(HEADS // 4):
            taps = probs_ref[rows, pl.ds(group * 128, 128)].astype(F32)
            taps = jnp.concatenate([taps, jnp.zeros((BLOCK, BLOCK), F32)], axis=1)
            band = pltpu.roll(taps, 1, 1, stride=1, stride_axis=0)
            for pair in range(2):
                lanes = pl.ds((group * 2 + pair) * 128, 128)
                halves = []
                for head in (2 * pair, 2 * pair + 1):
                    mine = (offset >= head * LANES) & (offset < (head + 1) * LANES)
                    own = jnp.where(mine, band, 0.0).astype(BF16)
                    start = FRONT + block * BLOCK - LANES * head
                    halves.append(
                        jnp.dot(
                            own,
                            padded_ref[pl.ds(start, 2 * BLOCK), lanes],
                            preferred_element_type=F32,
                        )
                    )
                left = iota((BLOCK, 128), 1) < 64
                mixed = tokens_ref[rows, lanes].astype(F32) + jnp.where(left, halves[0], halves[1])
                mixed_ref[rows, lanes] = mixed
                square = square + mixed * mixed
        squares.append(square)
    for block in range(count // BLOCK):
        rows = pl.ds(block * BLOCK, BLOCK)
        mean = jnp.sum(squares[block], axis=1, keepdims=True) / width
        scale = lax.rsqrt(mean + EPS)
        normed_ref[rows, :] = (mixed_ref[rows, :] * scale * gain_ref[...].astype(F32)).astype(BF16)

    normed = normed_ref[...]
    onehot = jnp.where(ids_ref[...] == iota((count, experts), 1), 1.0, 0.0)
    earlier = jnp.where(iota((count, count), 0) > iota((count, count), 1), 1.0, 0.0).astype(BF16)
    before = jnp.dot(earlier, onehot.astype(BF16), preferred_element_type=F32)
    slot_ref[...] = slots_of(onehot, before, capacity_row_ref[...].astype(F32), depth, 1)
    gates = jnp.dot(normed, router_ref[...], preferred_element_type=F32)
    gate_ref[...] = jax.nn.sigmoid(jnp.sum(gates * onehot, axis=1, keepdims=True))

    onehot_row = jnp.where(ids_row_ref[...] == iota((experts, count), 0), 1.0, 0.0)
    later = jnp.where(iota((count, count), 0) < iota((count, count), 1), 1.0, 0.0).astype(BF16)
    before_row = jnp.dot(onehot_row.astype(BF16), later, preferred_element_type=F32)
    slot_row = slots_of(onehot_row, before_row, capacity_ref[...].astype(F32), depth, 0)
    select = jnp.where(iota((experts * depth, count), 0) == slot_row, 1.0, 0.0).astype(BF16)
    packed_ref[...] = jnp.dot(select, normed, preferred_element_type=F32).astype(BF16)


def combine_kernel(mixed_ref, gate_ref, slot_ref, back_ref, out_ref):
    count = mixed_ref.shape[0]
    slots = back_ref.shape[0]
    select = jnp.where(slot_ref[...] == iota((count, slots), 1), 1.0, 0.0).astype(BF16)
    out = jnp.dot(select, back_ref[...], preferred_element_type=F32)
    out_ref[...] = (mixed_ref[...] + gate_ref[...] * out).astype(BF16)


def expert_kernel(pieces, rows_ref, *refs):
    weights, out_ref = refs[: 3 * pieces], refs[3 * pieces]
    rows = rows_ref[...]
    total = None
    for piece in range(pieces):
        gate_ref, up_ref, down_ref = weights[3 * piece : 3 * piece + 3]
        gated = jnp.dot(rows, gate_ref[...], preferred_element_type=F32)
        lifted = jnp.dot(rows, up_ref[...], preferred_element_type=F32)
        act = (gated / (1.0 + jnp.exp(-gated)) * lifted).astype(BF16)
        part = lax.dot_general(
            act, down_ref[...], (((1,), (1,)), ((), ())), preferred_element_type=F32
        )
        total = part if total is None else total + part
    out_ref[...] = total.astype(out_ref.dtype)


def call(kernel, out_shape, scratch=(), flops=0, moved=0):
    return pl.pallas_call(
        kernel,
        out_shape=out_shape,
        scratch_shapes=scratch,
        compiler_params=pltpu.CompilerParams(vmem_limit_bytes=40 * 1024 * 1024),
        cost_estimate=pl.CostEstimate(flops=flops, bytes_accessed=moved, transcendentals=0),
    )


def shape(dims, dtype):
    return jax.ShapeDtypeStruct(dims, dtype)


def on_device(
    tokens,
    expert_ids,
    expert_capacity,
    kernel_weight,
    norm_gain,
    router,
    expert_gate,
    expert_up,
    expert_down,
):
    local = tokens[0]
    count, width = local.shape
    experts = expert_capacity.shape[0]
    depth = max(2, 2 * count // experts)
    slots = experts * depth
    splits = lax.axis_size("blk")
    blocks = lax.axis_size("seq")
    groups = splits // 2
    partner = [(i, i ^ 1) for i in range(splits)]

    def turned(array, step):
        return lax.ppermute(
            array, "blk", [(i, (i + 2 * step) % splits) for i in range(splits)]
        )

    forward = [(i, i + 1) for i in range(blocks - 1)]
    backward = [(target, source) for source, target in forward]
    low = lax.ppermute(local[count - HALO :], "seq", forward)
    high = lax.ppermute(local[:HALO], "seq", backward)
    weights = [expert_gate[0], expert_up[0], expert_down[0]]
    for step in range(1, groups):
        weights += [turned(expert_gate[0], step), turned(expert_up[0], step), turned(expert_down[0], step)]

    probs = call(
        probs_kernel, shape((count, HEADS * LANES), BF16), flops=2 * count * width * 512 * 4, moved=1 << 21
    )(local, kernel_weight)
    ids = expert_ids[0]
    mixed, packed, gate, slot = call(
        functools.partial(mix_kernel, depth),
        (
            shape((count, width), F32),
            shape((slots, width), BF16),
            shape((count, 1), F32),
            shape((count, 1), jnp.int32),
        ),
        scratch=(
            pltpu.VMEM((FRONT + count + BLOCK, width), BF16),
            pltpu.VMEM((count, width), BF16),
        ),
        flops=1 << 31,
        moved=1 << 22,
    )(
        local,
        low,
        high,
        probs,
        ids.reshape(1, count),
        ids,
        expert_capacity[:, None],
        expert_capacity[None, :],
        norm_gain[None, :],
        router,
    )
    arrived = lax.all_to_all(
        packed.reshape(experts, depth, width), "seq", split_axis=0, concat_axis=0, tiled=True
    )
    rows = arrived.reshape(-1, width)
    other = lax.ppermute(rows, "blk", partner)
    total = rows.shape[0]
    flops = 6 * total * width * weights[0].shape[1] * groups
    other_part = call(
        functools.partial(expert_kernel, groups), shape((total, width), BF16), flops=flops, moved=1 << 23
    )(other, *weights)
    back_part = lax.ppermute(other_part, "blk", partner)
    own_part = call(
        functools.partial(expert_kernel, groups), shape((total, width), F32), flops=flops, moved=1 << 23
    )(rows, *weights)
    sent = (own_part + back_part.astype(F32)).astype(BF16).reshape(arrived.shape)
    back = lax.all_to_all(sent, "seq", split_axis=0, concat_axis=0, tiled=True).reshape(slots, width)
    result = call(combine_kernel, shape((count, width), BF16), flops=1 << 28, moved=1 << 22)(
        mixed, gate, slot, back
    )
    return result[None]


def solution(mesh):
    placed = (
        P("blk", "seq", None),
        P("blk", "seq", None),
        P(),
        P(),
        P(),
        P(),
        P("seq", None, "blk"),
        P("seq", None, "blk"),
        P("seq", None, "blk"),
    )
    return jax.shard_map(
        on_device, mesh=mesh, in_specs=placed, out_specs=P("blk", "seq", None), check_vma=False
    )
```

```python
import functools

import jax
import jax.numpy as jnp
from jax import lax
from jax.experimental import pallas as pl
from jax.experimental.pallas import tpu as pltpu
from jax.sharding import PartitionSpec as P

HEADS = 16
TAPS = 31
LANES = 32
HALO = 16
FRONT = 96
BLOCK = 128
EPS = 1e-06

VMEM = pl.BlockSpec(memory_space=pltpu.VMEM)
F32 = jnp.float32
BF16 = jnp.bfloat16


def iota(shape, dim):
    return lax.broadcasted_iota(jnp.int32, shape, dim)


def probs_kernel(tokens_ref, weight_ref, probs_ref):
    count = tokens_ref.shape[0]
    columns = weight_ref.shape[1]
    row = iota((columns, HEADS * LANES), 0)
    column = iota((columns, HEADS * LANES), 1)
    tap = column % LANES
    spread = jnp.where((column // LANES * TAPS + tap == row) & (tap < TAPS), 1.0, 0.0).astype(BF16)
    weight = jnp.dot(weight_ref[...], spread, preferred_element_type=F32).astype(BF16)
    logits = jnp.dot(tokens_ref[...], weight, preferred_element_type=F32)
    logits = logits.T.reshape(HEADS, LANES, count)
    used = iota(logits.shape, 1) < TAPS
    logits = jnp.where(used, logits, -3e38)
    top = jnp.max(logits, axis=1, keepdims=True)
    powers = jnp.exp(logits - top)
    probs = powers / jnp.sum(powers, axis=1, keepdims=True)
    probs_ref[...] = probs.reshape(HEADS * LANES, count).T.astype(BF16)


def slots_of(onehot, before, capacity, place, depth, axis):
    kept = jnp.sum(onehot * (before < capacity).astype(F32), axis=axis, keepdims=True) > 0.5
    apart = iota(onehot.shape, axis) ^ place
    first = ((apart >> 1) + (apart & 1) * (onehot.shape[axis] // 2)) * depth
    slot = jnp.sum(onehot * (first.astype(F32) + before), axis=axis, keepdims=True)
    return jnp.where(kept, slot, -1.0).astype(jnp.int32)


def mix_kernel(
    depth,
    tokens_ref,
    low_ref,
    high_ref,
    probs_ref,
    ids_row_ref,
    ids_ref,
    capacity_ref,
    capacity_row_ref,
    place_ref,
    gain_ref,
    router_ref,
    mixed_ref,
    packed_ref,
    gate_ref,
    slot_ref,
    padded_ref,
    normed_ref,
):
    count, width = tokens_ref.shape
    experts = capacity_ref.shape[0]
    padded_ref[pl.ds(0, FRONT), :] = jnp.zeros((FRONT, width), BF16)
    padded_ref[pl.ds(FRONT, HALO), :] = low_ref[...]
    padded_ref[pl.ds(FRONT + HALO, count), :] = tokens_ref[...]
    padded_ref[pl.ds(FRONT + HALO + count, HALO), :] = high_ref[...]
    after = FRONT + 2 * HALO + count
    padded_ref[pl.ds(after, padded_ref.shape[0] - after), :] = jnp.zeros(
        (padded_ref.shape[0] - after, width), BF16
    )
    offset = iota((BLOCK, 2 * BLOCK), 1) - iota((BLOCK, 2 * BLOCK), 0) - 1
    squares = []
    for block in range(count // BLOCK):
        rows = pl.ds(block * BLOCK, BLOCK)
        square = jnp.zeros((BLOCK, 128), F32)
        for group in range(HEADS // 4):
            taps = probs_ref[rows, pl.ds(group * 128, 128)].astype(F32)
            taps = jnp.concatenate([taps, jnp.zeros((BLOCK, BLOCK), F32)], axis=1)
            band = pltpu.roll(taps, 1, 1, stride=1, stride_axis=0)
            for pair in range(2):
                lanes = pl.ds((group * 2 + pair) * 128, 128)
                halves = []
                for head in (2 * pair, 2 * pair + 1):
                    mine = (offset >= head * LANES) & (offset < (head + 1) * LANES)
                    own = jnp.where(mine, band, 0.0).astype(BF16)
                    start = FRONT + block * BLOCK - LANES * head
                    halves.append(
                        jnp.dot(
                            own,
                            padded_ref[pl.ds(start, 2 * BLOCK), lanes],
                            preferred_element_type=F32,
                        )
                    )
                left = iota((BLOCK, 128), 1) < 64
                mixed = tokens_ref[rows, lanes].astype(F32) + jnp.where(left, halves[0], halves[1])
                mixed_ref[rows, lanes] = mixed
                square = square + mixed * mixed
        squares.append(square)
    for block in range(count // BLOCK):
        rows = pl.ds(block * BLOCK, BLOCK)
        mean = jnp.sum(squares[block], axis=1, keepdims=True) / width
        scale = lax.rsqrt(mean + EPS)
        normed_ref[rows, :] = (mixed_ref[rows, :] * scale * gain_ref[...].astype(F32)).astype(BF16)

    normed = normed_ref[...]
    onehot = jnp.where(ids_ref[...] == iota((count, experts), 1), 1.0, 0.0)
    earlier = jnp.where(iota((count, count), 0) > iota((count, count), 1), 1.0, 0.0).astype(BF16)
    before = jnp.dot(earlier, onehot.astype(BF16), preferred_element_type=F32)
    slot_ref[...] = slots_of(onehot, before, capacity_row_ref[...].astype(F32), place_ref[...], depth, 1)
    gates = jnp.dot(normed, router_ref[...], preferred_element_type=F32)
    gate_ref[...] = jax.nn.sigmoid(jnp.sum(gates * onehot, axis=1, keepdims=True))

    onehot_row = jnp.where(ids_row_ref[...] == iota((experts, count), 0), 1.0, 0.0)
    later = jnp.where(iota((count, count), 0) < iota((count, count), 1), 1.0, 0.0).astype(BF16)
    before_row = jnp.dot(onehot_row.astype(BF16), later, preferred_element_type=F32)
    slot_row = slots_of(onehot_row, before_row, capacity_ref[...].astype(F32), place_ref[...], depth, 0)
    select = jnp.where(iota((experts * depth, count), 0) == slot_row, 1.0, 0.0).astype(BF16)
    packed = jnp.dot(select, normed, preferred_element_type=F32).astype(BF16)
    packed_ref[...] = packed.reshape(packed_ref.shape)


def combine_kernel(mixed_ref, gate_ref, slot_ref, returned_ref, handed_ref, out_ref):
    count = mixed_ref.shape[0]
    half = returned_ref.shape[0]
    slot = slot_ref[...]
    near = jnp.where(slot == iota((count, half), 1), 1.0, 0.0).astype(BF16)
    cross = jnp.where(slot == iota((count, half), 1) + half, 1.0, 0.0).astype(BF16)
    out = jnp.dot(near, returned_ref[...], preferred_element_type=F32)
    out = out + jnp.dot(cross, handed_ref[...], preferred_element_type=F32)
    out_ref[...] = (mixed_ref[...] + gate_ref[...] * out).astype(BF16)


def expert_kernel(pieces, own_ref, far_ref, *refs):
    weights = refs[: 3 * pieces]
    own_out_ref, far_out_ref, rows_ref, total_ref = refs[3 * pieces :]
    size = own_ref.shape[0]
    rows_ref[pl.ds(0, size), :] = own_ref[...]
    rows_ref[pl.ds(size, size), :] = far_ref[...]
    rows = rows_ref[...]
    for piece in range(pieces):
        gate_ref, up_ref, down_ref = weights[3 * piece : 3 * piece + 3]
        gated = jnp.dot(rows, gate_ref[...], preferred_element_type=F32)
        lifted = jnp.dot(rows, up_ref[...], preferred_element_type=F32)
        act = (gated / (1.0 + jnp.exp(-gated)) * lifted).astype(BF16)
        part = lax.dot_general(
            act, down_ref[...], (((1,), (1,)), ((), ())), preferred_element_type=F32
        )
        total_ref[...] = part if piece == 0 else total_ref[...] + part
    own_out_ref[...] = total_ref[pl.ds(0, size), :]
    far_out_ref[...] = total_ref[pl.ds(size, size), :].astype(BF16)


def call(kernel, out_shape, scratch=()):
    return pl.pallas_call(
        kernel,
        out_shape=out_shape,
        scratch_shapes=scratch,
        compiler_params=pltpu.CompilerParams(vmem_limit_bytes=40 * 1024 * 1024),
        cost_estimate=pl.CostEstimate(flops=0, bytes_accessed=0, transcendentals=0),
    )


def shape(dims, dtype):
    return jax.ShapeDtypeStruct(dims, dtype)


def on_device(
    tokens,
    expert_ids,
    expert_capacity,
    kernel_weight,
    norm_gain,
    router,
    expert_gate,
    expert_up,
    expert_down,
):
    local = tokens[0]
    count, width = local.shape
    experts = expert_capacity.shape[0]
    depth = max(2, 2 * count // experts)
    splits = lax.axis_size("blk")
    blocks = lax.axis_size("seq")
    pieces = splits // 2
    chips = blocks // 2

    def across(array, masks):
        pairs = [
            (split * blocks + block, (split ^ masks[block % 2]) * blocks + block)
            for split in range(splits)
            for block in range(blocks)
        ]
        return lax.ppermute(array, ("blk", "seq"), pairs)

    row_masks = (1, 2)
    weight_masks = [
        [mask for mask in range(1, splits) if not mask & row_mask] for row_mask in row_masks
    ]

    def to_chip(array, apart):
        return lax.ppermute(array, "seq", [(i, i ^ (2 * apart)) for i in range(blocks)])

    def to_core(array):
        return lax.ppermute(array, "seq", [(i, i ^ 1) for i in range(blocks)])

    forward = [(i, i + 1) for i in range(blocks - 1)]
    backward = [(target, source) for source, target in forward]
    weights = [expert_gate[0], expert_up[0], expert_down[0]]
    for masks in zip(*weight_masks, strict=True):
        gate, up = across(weights[0], masks), across(weights[1], masks)
        down = lax.optimization_barrier((weights[2], gate))[0]
        weights += [gate, up, across(down, masks)]
    low = lax.ppermute(local[count - HALO :], "seq", forward)
    high = lax.ppermute(local[:HALO], "seq", backward)

    probs = call(probs_kernel, shape((count, HEADS * LANES), BF16))(local, kernel_weight)
    ids = expert_ids[0]
    place = lax.axis_index("seq").astype(jnp.int32).reshape(1, 1)
    mixed, packed, gate, slot = call(
        functools.partial(mix_kernel, depth),
        (
            shape((count, width), F32),
            shape((2, chips, depth, width), BF16),
            shape((count, 1), F32),
            shape((count, 1), jnp.int32),
        ),
        scratch=(
            pltpu.VMEM((FRONT + count + BLOCK, width), BF16),
            pltpu.VMEM((count, width), BF16),
        ),
    )(
        local,
        low,
        high,
        probs,
        ids.reshape(1, count),
        ids,
        expert_capacity[:, None],
        expert_capacity[None, :],
        place,
        norm_gain[None, :],
        router,
    )
    crossed = to_core(packed[1])
    both = jnp.concatenate([packed[0], crossed], axis=1)
    size = 2 * depth
    backs = []
    for apart in range(chips):
        rows = to_chip(both[apart], apart) if apart else both[apart]
        own, other = call(
            functools.partial(expert_kernel, pieces),
            (shape((size, width), F32), shape((size, width), BF16)),
            scratch=(pltpu.VMEM((2 * size, width), BF16), pltpu.VMEM((2 * size, width), F32)),
        )(rows, across(rows, row_masks), *weights)
        done = (own + across(other, row_masks).astype(F32)).astype(BF16)
        backs.append(to_chip(done, apart) if apart else done)
    back = jnp.stack(backs).reshape(chips, 2, depth, width)
    returned = back[:, 0].reshape(chips * depth, width)
    handed = to_core(back[:, 1].reshape(chips * depth, width))
    result = call(combine_kernel, shape((count, width), BF16))(mixed, gate, slot, returned, handed)
    return result[None]


def solution(mesh):
    placed = (
        P("blk", "seq", None),
        P("blk", "seq", None),
        P(),
        P(),
        P(),
        P(),
        P("seq", None, "blk"),
        P("seq", None, "blk"),
        P("seq", None, "blk"),
    )
    return jax.shard_map(
        on_device, mesh=mesh, in_specs=placed, out_specs=P("blk", "seq", None), check_vma=False
    )
```

```python
import functools

import jax
import jax.numpy as jnp
from jax import lax
from jax.experimental import pallas as pl
from jax.experimental.pallas import tpu as pltpu
from jax.sharding import PartitionSpec as P

HEADS = 16
TAPS = 31
LANES = 32
HALO = 16
FRONT = 96
BLOCK = 128
EPS = 1e-06

VMEM = pl.BlockSpec(memory_space=pltpu.VMEM)
HBM = pl.BlockSpec(memory_space=pl.ANY)
F32 = jnp.float32
BF16 = jnp.bfloat16


def iota(shape, dim):
    return lax.broadcasted_iota(jnp.int32, shape, dim)


def probs_kernel(
    depth,
    tokens_ref,
    weight_ref,
    ids_ref,
    place_ref,
    capacity_hbm,
    gain_hbm,
    router_hbm,
    probs_ref,
    onehot_ref,
    slot_ref,
    slot_row_ref,
    gain_ref,
    router_ref,
    capacity_ref,
    sems,
):
    copies = [
        pltpu.make_async_copy(source, target, sems.at[index])
        for index, (source, target) in enumerate(
            ((capacity_hbm, capacity_ref), (gain_hbm, gain_ref), (router_hbm, router_ref))
        )
    ]
    for copy in copies:
        copy.start()
    count = tokens_ref.shape[0]
    columns = weight_ref.shape[0]
    row = iota((HEADS * LANES, columns), 0)
    column = iota((HEADS * LANES, columns), 1)
    tap = row % LANES
    spread = jnp.where((row // LANES * TAPS + tap == column) & (tap < TAPS), 1.0, 0.0).astype(BF16)
    weight = jnp.dot(spread, weight_ref[...], preferred_element_type=F32).astype(BF16)
    logits = lax.dot_general(
        weight, tokens_ref[...], (((1,), (1,)), ((), ())), preferred_element_type=F32
    )
    logits = logits.reshape(HEADS, LANES, count)
    logits = jnp.where(iota(logits.shape, 1) < TAPS, logits, -3e38)
    top = jnp.max(logits, axis=1, keepdims=True)
    powers = jnp.exp(logits - top)
    probs = powers / jnp.sum(powers, axis=1, keepdims=True)
    probs_ref[...] = probs.reshape(HEADS * LANES, count).T.astype(BF16)

    for copy in copies:
        copy.wait()
    experts = router_ref.shape[0]
    expert = iota((experts, count), 0)
    onehot = jnp.where(ids_ref[...] == expert, 1.0, 0.0)
    later = jnp.where(iota((count, count), 0) < iota((count, count), 1), 1.0, 0.0).astype(BF16)
    before = jnp.dot(onehot.astype(BF16), later, preferred_element_type=F32)
    capacity = jnp.zeros((experts, count), jnp.int32)
    for index in range(experts):
        capacity = jnp.where(expert == index, capacity_ref[index], capacity)
    kept = jnp.sum(onehot * (before < capacity.astype(F32)).astype(F32), axis=0, keepdims=True)
    apart = expert ^ place_ref[0]
    first = ((apart >> 1) + (apart & 1) * (experts // 2)) * depth
    slot = jnp.sum(onehot * (first.astype(F32) + before), axis=0, keepdims=True)
    slot = jnp.where(kept > 0.5, slot, -1.0)
    slot_row_ref[...] = slot.astype(jnp.int32)
    slot_ref[...] = jnp.broadcast_to(slot, (8, count)).T.astype(jnp.int32)
    onehot_ref[...] = onehot.T


def mix_kernel(
    tokens_ref,
    low_ref,
    high_ref,
    probs_ref,
    onehot_ref,
    slot_row_ref,
    gain_ref,
    router_ref,
    mixed_ref,
    packed_ref,
    gate_ref,
    padded_ref,
    normed_ref,
):
    count, width = tokens_ref.shape
    padded_ref[pl.ds(0, FRONT), :] = jnp.zeros((FRONT, width), BF16)
    padded_ref[pl.ds(FRONT, HALO), :] = low_ref[...]
    padded_ref[pl.ds(FRONT + HALO, count), :] = tokens_ref[...]
    padded_ref[pl.ds(FRONT + HALO + count, HALO), :] = high_ref[...]
    after = FRONT + 2 * HALO + count
    padded_ref[pl.ds(after, padded_ref.shape[0] - after), :] = jnp.zeros(
        (padded_ref.shape[0] - after, width), BF16
    )
    offset = iota((BLOCK, 2 * BLOCK), 1) - iota((BLOCK, 2 * BLOCK), 0) - 1
    squares = []
    for block in range(count // BLOCK):
        rows = pl.ds(block * BLOCK, BLOCK)
        square = jnp.zeros((BLOCK, 128), F32)
        for group in range(HEADS // 4):
            taps = probs_ref[rows, pl.ds(group * 128, 128)].astype(F32)
            taps = jnp.concatenate([taps, jnp.zeros((BLOCK, BLOCK), F32)], axis=1)
            band = pltpu.roll(taps, 1, 1, stride=1, stride_axis=0)
            for pair in range(2):
                lanes = pl.ds((group * 2 + pair) * 128, 128)
                halves = []
                for head in (2 * pair, 2 * pair + 1):
                    mine = (offset >= head * LANES) & (offset < (head + 1) * LANES)
                    own = jnp.where(mine, band, 0.0).astype(BF16)
                    start = FRONT + block * BLOCK - LANES * head
                    halves.append(
                        jnp.dot(
                            own,
                            padded_ref[pl.ds(start, 2 * BLOCK), lanes],
                            preferred_element_type=F32,
                        )
                    )
                left = iota((BLOCK, 128), 1) < 64
                mixed = tokens_ref[rows, lanes].astype(F32) + jnp.where(left, halves[0], halves[1])
                mixed_ref[rows, lanes] = mixed
                square = square + mixed * mixed
        squares.append(square)
    gain = gain_ref[...].astype(F32)
    for block in range(count // BLOCK):
        rows = pl.ds(block * BLOCK, BLOCK)
        mean = jnp.sum(squares[block], axis=1, keepdims=True) / width
        scale = lax.rsqrt(mean + EPS)
        normed_ref[rows, :] = (mixed_ref[rows, :] * scale * gain).astype(BF16)

    normed = normed_ref[...]
    slots = packed_ref.shape[0] * packed_ref.shape[1] * packed_ref.shape[2]
    select = jnp.where(iota((slots, count), 0) == slot_row_ref[...], 1.0, 0.0).astype(BF16)
    packed = jnp.dot(select, normed, preferred_element_type=F32).astype(BF16)
    packed_ref[...] = packed.reshape(packed_ref.shape)
    gates = lax.dot_general(
        normed, router_ref[...], (((1,), (1,)), ((), ())), preferred_element_type=F32
    )
    gate_ref[...] = jax.nn.sigmoid(jnp.sum(gates * onehot_ref[...], axis=1, keepdims=True))


def combine_kernel(mixed_ref, gate_ref, slot_ref, returned_ref, handed_ref, out_ref):
    count = mixed_ref.shape[0]
    half = returned_ref.shape[0]
    slot = slot_ref[:, :1]
    near = jnp.where(slot == iota((count, half), 1), 1.0, 0.0).astype(BF16)
    cross = jnp.where(slot == iota((count, half), 1) + half, 1.0, 0.0).astype(BF16)
    out = jnp.dot(near, returned_ref[...], preferred_element_type=F32)
    out = out + jnp.dot(cross, handed_ref[...], preferred_element_type=F32)
    out_ref[...] = (mixed_ref[...] + gate_ref[...] * out).astype(BF16)


def act_kernel(pieces, groups, *refs):
    rows_refs, weights = refs[: 2 * groups], refs[2 * groups : 2 * groups + 2 * pieces]
    acts, rows_ref = refs[2 * groups + 2 * pieces : -1], refs[-1]
    size = rows_refs[0].shape[0]
    for index, ref in enumerate(rows_refs):
        rows_ref[pl.ds(index * size, size), :] = ref[...]
    rows = rows_ref[...]
    for piece in range(pieces):
        gate_ref, up_ref = weights[2 * piece : 2 * piece + 2]
        gated = jnp.dot(rows, gate_ref[...], preferred_element_type=F32)
        lifted = jnp.dot(rows, up_ref[...], preferred_element_type=F32)
        acts[piece][...] = (gated / (1.0 + jnp.exp(-gated)) * lifted).astype(BF16)


def down_kernel(pieces, first, *refs):
    acts, downs, (own_ref, far_ref) = refs[:pieces], refs[pieces : 2 * pieces], refs[2 * pieces :]
    size = own_ref.shape[0]
    total = None
    for act_ref, down_ref in zip(acts, downs, strict=True):
        part = lax.dot_general(
            act_ref[pl.ds(first, 2 * size), :],
            down_ref[...],
            (((1,), (1,)), ((), ())),
            preferred_element_type=F32,
        )
        total = part if total is None else total + part
    own_ref[...] = total[:size]
    far_ref[...] = total[size:].astype(BF16)


def add_kernel(own_ref, other_ref, out_ref):
    out_ref[...] = (own_ref[...] + other_ref[...].astype(F32)).astype(BF16)


def split_kernel(back_ref, returned_ref, handed_ref):
    half = returned_ref.shape[0]
    returned_ref[...] = back_ref[pl.ds(0, half), :]
    handed_ref[...] = back_ref[pl.ds(half, half), :]


ADD_COST = 8 << 20
SPLIT_COST = 8 << 20


def call(kernel, out_shape, scratch=(), in_specs=None, cost=0):
    extra = {} if in_specs is None else {"in_specs": in_specs}
    return pl.pallas_call(
        kernel,
        out_shape=out_shape,
        scratch_shapes=scratch,
        **extra,
        compiler_params=pltpu.CompilerParams(vmem_limit_bytes=24 * 1024 * 1024),
        cost_estimate=pl.CostEstimate(flops=0, bytes_accessed=cost, transcendentals=0),
    )


def shape(dims, dtype):
    return jax.ShapeDtypeStruct(dims, dtype)


def on_device(
    tokens,
    expert_ids,
    expert_capacity,
    kernel_weight,
    norm_gain,
    router,
    expert_gate,
    expert_up,
    expert_down,
):
    local = tokens[0]
    count, width = local.shape
    experts = expert_capacity.shape[0]
    depth = max(2, 2 * count // experts)
    splits = lax.axis_size("blk")
    blocks = lax.axis_size("seq")
    pieces = splits // 2
    chips = blocks // 2

    def across(array, masks):
        pairs = [
            (split * blocks + block, (split ^ masks[block % 2]) * blocks + block)
            for split in range(splits)
            for block in range(blocks)
        ]
        return lax.ppermute(array, ("blk", "seq"), pairs)

    def after(array, earlier):
        return lax.optimization_barrier((array, earlier))[0]

    row_masks = (1, 2)
    weight_masks = [
        [mask for mask in range(1, splits) if not mask & row_mask] for row_mask in row_masks
    ]

    def to_chip(array, apart):
        return lax.ppermute(array, "seq", [(i, i ^ (2 * apart)) for i in range(blocks)])

    def to_core(array):
        return lax.ppermute(array, "seq", [(i, i ^ 1) for i in range(blocks)])

    forward = [(i, i + 1) for i in range(blocks - 1)]
    backward = [(target, source) for source, target in forward]
    inner, downs = [expert_gate[0], expert_up[0]], [expert_down[0]]
    for masks in zip(*weight_masks, strict=True):
        inner += [across(array, masks) for array in inner[:2]]
        downs.append(across(after(downs[0], inner[-2]), masks))
    low = lax.ppermute(local[count - HALO :], "seq", forward)
    high = lax.ppermute(local[:HALO], "seq", backward)

    place = lax.axis_index("seq").astype(jnp.int32).reshape(1)
    probs, onehot, slot, slot_row, gain, columns = call(
        functools.partial(probs_kernel, depth),
        (
            shape((count, HEADS * LANES), BF16),
            shape((count, experts), F32),
            shape((count, 8), jnp.int32),
            shape((1, count), jnp.int32),
            shape((1, width), BF16),
            shape((experts, width), BF16),
        ),
        scratch=(pltpu.SMEM((experts,), jnp.int32), pltpu.SemaphoreType.DMA((3,))),
        in_specs=[VMEM, VMEM, VMEM, pl.BlockSpec(memory_space=pltpu.SMEM), HBM, HBM, HBM],
    )(
        local,
        kernel_weight.T,
        expert_ids[0].reshape(1, count),
        place,
        expert_capacity,
        norm_gain[None, :],
        router.T,
    )
    mixed, packed, gate = call(
        mix_kernel,
        (
            shape((count, width), F32),
            shape((2, chips, depth, width), BF16),
            shape((count, 1), F32),
        ),
        scratch=(
            pltpu.VMEM((FRONT + count + BLOCK, width), BF16),
            pltpu.VMEM((count, width), BF16),
        ),
    )(local, low, high, probs, onehot, slot_row, gain, columns)
    crossed = to_core(packed[1])
    both = jnp.concatenate([packed[0], crossed], axis=1)
    size = 2 * depth
    near = list(range(chips // 2))
    order = [apart for apart in reversed(range(chips)) if apart not in near]
    hidden = inner[0].shape[1]
    rows, sums = [None] * chips, [None] * chips

    def arrive(apart, earlier):
        array = both[apart] if earlier is None else after(both[apart], earlier)
        rows[apart] = to_chip(array, apart) if apart else array

    def work(apart, earlier, behind=None):
        if earlier is not None:
            rows[apart] = after(rows[apart], earlier)
        far = across(rows[apart], row_masks)
        own = rows[apart] if behind is None else after(rows[apart], behind)
        acts = call(
            functools.partial(act_kernel, pieces, 1),
            [shape((2 * size, hidden), BF16)] * pieces,
            scratch=(pltpu.VMEM((2 * size, width), BF16),),
        )(own, far, *inner)
        sums[apart] = call(
            functools.partial(down_kernel, pieces, 0),
            (shape((size, width), F32), shape((size, width), BF16)),
        )(*acts, *downs)

    returned, handed = [None] * chips, [None] * chips

    def finish(apart, earlier=None, cost=0):
        own, other = sums[apart]
        done = call(add_kernel, shape((size, width), BF16), cost=cost)(own, across(other, row_masks))
        sent = done if earlier is None else after(done, earlier)
        back = to_chip(sent, apart) if apart else sent
        returned[apart], handed[apart] = call(
            split_kernel, [shape((depth, width), BF16)] * 2, cost=SPLIT_COST
        )(back)
        return done

    for index, apart in enumerate(order):
        arrive(apart, rows[order[index - 1]] if index else None)
        if index == 0:
            work(apart, None)
            first = finish(apart, None, ADD_COST)
        else:
            work(apart, sums[order[index - 1]][1], first)
            finish(apart, returned[order[index - 1]])
    for apart in near:
        arrive(apart, None)
        work(apart, sums[order[0]][1])
        finish(apart)
    returned = jnp.concatenate(returned)
    handed = to_core(jnp.concatenate(handed))
    result = call(combine_kernel, shape((count, width), BF16))(mixed, gate, slot, returned, handed)
    return result[None]


def solution(mesh):
    placed = (
        P("blk", "seq", None),
        P("blk", "seq", None),
        P(),
        P(),
        P(),
        P(),
        P("seq", None, "blk"),
        P("seq", None, "blk"),
        P("seq", None, "blk"),
    )
    return jax.shard_map(
        on_device, mesh=mesh, in_specs=placed, out_specs=P("blk", "seq", None), check_vma=False
    )
```

```python
import functools

import jax
import jax.numpy as jnp
from jax import lax
from jax.experimental import pallas as pl
from jax.experimental.pallas import tpu as pltpu
from jax.sharding import PartitionSpec as P

HEADS = 16
TAPS = 31
LANES = 32
HALO = 16
FRONT = 96
BLOCK = 128
EPS = 1e-06

VMEM = pl.BlockSpec(memory_space=pltpu.VMEM)
HBM = pl.BlockSpec(memory_space=pl.ANY)
F32 = jnp.float32
BF16 = jnp.bfloat16


def iota(shape, dim):
    return lax.broadcasted_iota(jnp.int32, shape, dim)


def probs_kernel(
    depth,
    tokens_ref,
    weight_ref,
    ids_ref,
    place_ref,
    capacity_hbm,
    gain_hbm,
    router_hbm,
    probs_ref,
    onehot_ref,
    slot_ref,
    slot_row_ref,
    gain_ref,
    router_ref,
    capacity_ref,
    sems,
):
    copies = [
        pltpu.make_async_copy(source, target, sems.at[index])
        for index, (source, target) in enumerate(
            ((capacity_hbm, capacity_ref), (gain_hbm, gain_ref), (router_hbm, router_ref))
        )
    ]
    for copy in copies:
        copy.start()
    count = tokens_ref.shape[0]
    columns = weight_ref.shape[0]
    row = iota((HEADS * LANES, columns), 0)
    column = iota((HEADS * LANES, columns), 1)
    tap = row % LANES
    spread = jnp.where((row // LANES * TAPS + tap == column) & (tap < TAPS), 1.0, 0.0).astype(BF16)
    weight = jnp.dot(spread, weight_ref[...], preferred_element_type=F32).astype(BF16)
    logits = lax.dot_general(
        weight, tokens_ref[...], (((1,), (1,)), ((), ())), preferred_element_type=F32
    )
    logits = logits.reshape(HEADS, LANES, count)
    logits = jnp.where(iota(logits.shape, 1) < TAPS, logits, -3e38)
    top = jnp.max(logits, axis=1, keepdims=True)
    powers = jnp.exp(logits - top)
    probs = powers / jnp.sum(powers, axis=1, keepdims=True)
    probs_ref[...] = probs.reshape(HEADS * LANES, count).T.astype(BF16)

    for copy in copies:
        copy.wait()
    experts = router_ref.shape[0]
    expert = iota((experts, count), 0)
    onehot = jnp.where(ids_ref[...] == expert, 1.0, 0.0)
    later = jnp.where(iota((count, count), 0) < iota((count, count), 1), 1.0, 0.0).astype(BF16)
    before = jnp.dot(onehot.astype(BF16), later, preferred_element_type=F32)
    capacity = jnp.zeros((experts, count), jnp.int32)
    for index in range(experts):
        capacity = jnp.where(expert == index, capacity_ref[index], capacity)
    kept = jnp.sum(onehot * (before < capacity.astype(F32)).astype(F32), axis=0, keepdims=True)
    apart = expert ^ place_ref[0]
    first = ((apart >> 1) + (apart & 1) * (experts // 2)) * depth
    slot = jnp.sum(onehot * (first.astype(F32) + before), axis=0, keepdims=True)
    slot = jnp.where(kept > 0.5, slot, -1.0)
    slot_row_ref[...] = slot.astype(jnp.int32)
    slot_ref[...] = jnp.broadcast_to(slot, (8, count)).T.astype(jnp.int32)
    onehot_ref[...] = onehot.T


def mix_kernel(
    tokens_ref,
    low_ref,
    high_ref,
    probs_ref,
    onehot_ref,
    slot_row_ref,
    gain_ref,
    router_ref,
    mixed_ref,
    packed_ref,
    gate_ref,
    padded_ref,
    normed_ref,
):
    count, width = tokens_ref.shape
    padded_ref[pl.ds(0, FRONT), :] = jnp.zeros((FRONT, width), BF16)
    padded_ref[pl.ds(FRONT, HALO), :] = low_ref[...]
    padded_ref[pl.ds(FRONT + HALO, count), :] = tokens_ref[...]
    padded_ref[pl.ds(FRONT + HALO + count, HALO), :] = high_ref[...]
    after = FRONT + 2 * HALO + count
    padded_ref[pl.ds(after, padded_ref.shape[0] - after), :] = jnp.zeros(
        (padded_ref.shape[0] - after, width), BF16
    )
    offset = iota((BLOCK, 2 * BLOCK), 1) - iota((BLOCK, 2 * BLOCK), 0) - 1
    squares = []
    for block in range(count // BLOCK):
        rows = pl.ds(block * BLOCK, BLOCK)
        square = jnp.zeros((BLOCK, 128), F32)
        for group in range(HEADS // 4):
            taps = probs_ref[rows, pl.ds(group * 128, 128)].astype(F32)
            taps = jnp.concatenate([taps, jnp.zeros((BLOCK, BLOCK), F32)], axis=1)
            band = pltpu.roll(taps, 1, 1, stride=1, stride_axis=0)
            for pair in range(2):
                lanes = pl.ds((group * 2 + pair) * 128, 128)
                halves = []
                for head in (2 * pair, 2 * pair + 1):
                    mine = (offset >= head * LANES) & (offset < (head + 1) * LANES)
                    own = jnp.where(mine, band, 0.0).astype(BF16)
                    start = FRONT + block * BLOCK - LANES * head
                    halves.append(
                        jnp.dot(
                            own,
                            padded_ref[pl.ds(start, 2 * BLOCK), lanes],
                            preferred_element_type=F32,
                        )
                    )
                left = iota((BLOCK, 128), 1) < 64
                mixed = tokens_ref[rows, lanes].astype(F32) + jnp.where(left, halves[0], halves[1])
                mixed_ref[rows, lanes] = mixed
                square = square + mixed * mixed
        squares.append(square)
    gain = gain_ref[...].astype(F32)
    for block in range(count // BLOCK):
        rows = pl.ds(block * BLOCK, BLOCK)
        mean = jnp.sum(squares[block], axis=1, keepdims=True) / width
        scale = lax.rsqrt(mean + EPS)
        normed_ref[rows, :] = (mixed_ref[rows, :] * scale * gain).astype(BF16)

    normed = normed_ref[...]
    slots = packed_ref.shape[0] * packed_ref.shape[1] * packed_ref.shape[2]
    select = jnp.where(iota((slots, count), 0) == slot_row_ref[...], 1.0, 0.0).astype(BF16)
    packed = jnp.dot(select, normed, preferred_element_type=F32).astype(BF16)
    packed_ref[...] = packed.reshape(packed_ref.shape)
    gates = lax.dot_general(
        normed, router_ref[...], (((1,), (1,)), ((), ())), preferred_element_type=F32
    )
    gate_ref[...] = jax.nn.sigmoid(jnp.sum(gates * onehot_ref[...], axis=1, keepdims=True))


def combine_kernel(mixed_ref, gate_ref, slot_ref, returned_ref, handed_ref, out_ref):
    count = mixed_ref.shape[0]
    half = returned_ref.shape[0]
    slot = slot_ref[:, :1]
    near = jnp.where(slot == iota((count, half), 1), 1.0, 0.0).astype(BF16)
    cross = jnp.where(slot == iota((count, half), 1) + half, 1.0, 0.0).astype(BF16)
    out = jnp.dot(near, returned_ref[...], preferred_element_type=F32)
    out = out + jnp.dot(cross, handed_ref[...], preferred_element_type=F32)
    out_ref[...] = (mixed_ref[...] + gate_ref[...] * out).astype(BF16)


def act_kernel(pieces, groups, *refs):
    rows_refs, weights = refs[: 2 * groups], refs[2 * groups : 2 * groups + 2 * pieces]
    acts, rows_ref = refs[2 * groups + 2 * pieces : -1], refs[-1]
    size = rows_refs[0].shape[0]
    for index, ref in enumerate(rows_refs):
        rows_ref[pl.ds(index * size, size), :] = ref[...]
    rows = rows_ref[...]
    for piece in range(pieces):
        gate_ref, up_ref = weights[2 * piece : 2 * piece + 2]
        gated = jnp.dot(rows, gate_ref[...], preferred_element_type=F32)
        lifted = jnp.dot(rows, up_ref[...], preferred_element_type=F32)
        acts[piece][...] = (gated / (1.0 + jnp.exp(-gated)) * lifted).astype(BF16)


def down_kernel(pieces, first, *refs):
    acts, downs, (own_ref, far_ref) = refs[:pieces], refs[pieces : 2 * pieces], refs[2 * pieces :]
    size = own_ref.shape[0]
    total = None
    for act_ref, down_ref in zip(acts, downs, strict=True):
        part = lax.dot_general(
            act_ref[pl.ds(first, 2 * size), :],
            down_ref[...],
            (((1,), (1,)), ((), ())),
            preferred_element_type=F32,
        )
        total = part if total is None else total + part
    own_ref[...] = total[:size]
    far_ref[...] = total[size:].astype(BF16)


def add_kernel(own_ref, other_ref, out_ref):
    out_ref[...] = (own_ref[...] + other_ref[...].astype(F32)).astype(BF16)


def split_kernel(back_ref, returned_ref, handed_ref):
    half = returned_ref.shape[0]
    returned_ref[...] = back_ref[pl.ds(0, half), :]
    handed_ref[...] = back_ref[pl.ds(half, half), :]


def call(kernel, out_shape, scratch=(), in_specs=None):
    extra = {} if in_specs is None else {"in_specs": in_specs}
    return pl.pallas_call(
        kernel,
        out_shape=out_shape,
        scratch_shapes=scratch,
        **extra,
        compiler_params=pltpu.CompilerParams(vmem_limit_bytes=24 * 1024 * 1024),
        cost_estimate=pl.CostEstimate(flops=0, bytes_accessed=0, transcendentals=0),
    )


def shape(dims, dtype):
    return jax.ShapeDtypeStruct(dims, dtype)


def on_device(
    tokens,
    expert_ids,
    expert_capacity,
    kernel_weight,
    norm_gain,
    router,
    expert_gate,
    expert_up,
    expert_down,
):
    local = tokens[0]
    count, width = local.shape
    experts = expert_capacity.shape[0]
    depth = max(2, 2 * count // experts)
    splits = lax.axis_size("blk")
    blocks = lax.axis_size("seq")
    pieces = splits // 2
    chips = blocks // 2

    def across(array, masks):
        pairs = [
            (split * blocks + block, (split ^ masks[block % 2]) * blocks + block)
            for split in range(splits)
            for block in range(blocks)
        ]
        return lax.ppermute(array, ("blk", "seq"), pairs)

    def after(array, earlier):
        return lax.optimization_barrier((array, earlier))[0]

    row_masks = (1, 2)
    weight_masks = [
        [mask for mask in range(1, splits) if not mask & row_mask] for row_mask in row_masks
    ]

    def to_chip(array, apart):
        return lax.ppermute(array, "seq", [(i, i ^ (2 * apart)) for i in range(blocks)])

    def to_core(array):
        return lax.ppermute(array, "seq", [(i, i ^ 1) for i in range(blocks)])

    forward = [(i, i + 1) for i in range(blocks - 1)]
    backward = [(target, source) for source, target in forward]
    inner, downs = [expert_gate[0], expert_up[0]], [expert_down[0]]
    for masks in zip(*weight_masks, strict=True):
        inner += [across(array, masks) for array in inner[:2]]
        downs.append(across(after(downs[0], inner[-2]), masks))
    low = lax.ppermute(local[count - HALO :], "seq", forward)
    high = lax.ppermute(local[:HALO], "seq", backward)

    place = lax.axis_index("seq").astype(jnp.int32).reshape(1)
    probs, onehot, slot, slot_row, gain, columns = call(
        functools.partial(probs_kernel, depth),
        (
            shape((count, HEADS * LANES), BF16),
            shape((count, experts), F32),
            shape((count, 8), jnp.int32),
            shape((1, count), jnp.int32),
            shape((1, width), BF16),
            shape((experts, width), BF16),
        ),
        scratch=(pltpu.SMEM((experts,), jnp.int32), pltpu.SemaphoreType.DMA((3,))),
        in_specs=[VMEM, VMEM, VMEM, pl.BlockSpec(memory_space=pltpu.SMEM), HBM, HBM, HBM],
    )(
        local,
        kernel_weight.T,
        expert_ids[0].reshape(1, count),
        place,
        expert_capacity,
        norm_gain[None, :],
        router.T,
    )
    mixed, packed, gate = call(
        mix_kernel,
        (
            shape((count, width), F32),
            shape((2, chips, depth, width), BF16),
            shape((count, 1), F32),
        ),
        scratch=(
            pltpu.VMEM((FRONT + count + BLOCK, width), BF16),
            pltpu.VMEM((count, width), BF16),
        ),
    )(local, low, high, probs, onehot, slot_row, gain, columns)
    crossed = to_core(packed[1])
    both = jnp.concatenate([packed[0], crossed], axis=1)
    size = 2 * depth
    near = list(range(chips // 2))
    order = [apart for apart in reversed(range(chips)) if apart not in near]
    hidden = inner[0].shape[1]
    rows, sums = [None] * chips, [None] * chips

    def arrive(apart, earlier):
        array = both[apart] if earlier is None else after(both[apart], earlier)
        rows[apart] = to_chip(array, apart) if apart else array

    def work(apart, earlier, behind=None):
        if earlier is not None:
            rows[apart] = after(rows[apart], earlier)
        far = across(rows[apart], row_masks)
        own = rows[apart] if behind is None else after(rows[apart], behind)
        acts = call(
            functools.partial(act_kernel, pieces, 1),
            [shape((2 * size, hidden), BF16)] * pieces,
            scratch=(pltpu.VMEM((2 * size, width), BF16),),
        )(own, far, *inner)
        sums[apart] = call(
            functools.partial(down_kernel, pieces, 0),
            (shape((size, width), F32), shape((size, width), BF16)),
        )(*acts, *downs)

    returned, handed = [None] * chips, [None] * chips

    def finish(apart, earlier=None):
        own, other = sums[apart]
        done = call(add_kernel, shape((size, width), BF16))(own, across(other, row_masks))
        sent = done if earlier is None else after(done, earlier)
        back = to_chip(sent, apart) if apart else sent
        returned[apart], handed[apart] = call(
            split_kernel, [shape((depth, width), BF16)] * 2
        )(back)
        return done

    for index, apart in enumerate(order):
        arrive(apart, rows[order[index - 1]] if index else None)
        if index == 0:
            work(apart, tuple(inner[3::2]))
            first = finish(apart)
        else:
            work(apart, sums[order[index - 1]][1], first)
            finish(apart, returned[order[index - 1]])
    for apart in near:
        arrive(apart, None)
        work(apart, sums[order[0]][1])
        finish(apart)
    returned = jnp.concatenate(returned)
    handed = to_core(jnp.concatenate(handed))
    result = call(combine_kernel, shape((count, width), BF16))(mixed, gate, slot, returned, handed)
    return result[None]


def solution(mesh):
    placed = (
        P("blk", "seq", None),
        P("blk", "seq", None),
        P(),
        P(),
        P(),
        P(),
        P("seq", None, "blk"),
        P("seq", None, "blk"),
        P("seq", None, "blk"),
    )
    return jax.shard_map(
        on_device, mesh=mesh, in_specs=placed, out_specs=P("blk", "seq", None), check_vma=False
    )
```

```python
import functools

import jax
import jax.numpy as jnp
from jax import lax
from jax.experimental import pallas as pl
from jax.experimental.pallas import tpu as pltpu
from jax.sharding import PartitionSpec as P

HEADS = 16
TAPS = 31
LANES = 32
HALO = 16
FRONT = 96
BLOCK = 128
EPS = 1e-06

VMEM = pl.BlockSpec(memory_space=pltpu.VMEM)
HBM = pl.BlockSpec(memory_space=pltpu.HBM)
SMEM = pl.BlockSpec(memory_space=pltpu.SMEM)
F32 = jnp.float32
BF16 = jnp.bfloat16


def iota(shape, dim):
    return lax.broadcasted_iota(jnp.int32, shape, dim)


def fetch_kernel(place_ref, *refs):
    count = len(refs) // 2 - 2
    sources, targets, (near_ref, cross_ref, sems) = refs[:count], refs[count:-3], refs[-3:]
    half = sources[-1].shape[0] // 2
    sources = [*sources[:-1], *[sources[-1].at[pl.ds(first, half), :] for first in (0, half)]]
    copies = [
        pltpu.make_async_copy(source, target, sems.at[index])
        for index, (source, target) in enumerate(zip(sources, targets, strict=True))
    ]
    for copy in copies:
        copy.start()
    copies[0].wait()
    tokens_ref = targets[0]
    head = tokens_ref[pl.ds(0, HALO), :]
    tail = tokens_ref[pl.ds(tokens_ref.shape[0] - HALO, HALO), :]
    low_core = place_ref[0] % 2 == 0
    near_ref[...] = jnp.where(low_core, tail, head)
    cross_ref[...] = jnp.where(low_core, head, tail)
    for copy in copies[1:]:
        copy.wait()


def probs_kernel(
    depth,
    tokens_ref,
    weight_ref,
    ids_ref,
    capacity_ref,
    place_ref,
    probs_ref,
    onehot_ref,
    slot_ref,
    slot_row_ref,
):
    count = tokens_ref.shape[0]
    columns = weight_ref.shape[0]
    row = iota((HEADS * LANES, columns), 0)
    column = iota((HEADS * LANES, columns), 1)
    tap = row % LANES
    spread = jnp.where((row // LANES * TAPS + tap == column) & (tap < TAPS), 1.0, 0.0).astype(BF16)
    weight = jnp.dot(spread, weight_ref[...], preferred_element_type=F32).astype(BF16)
    logits = lax.dot_general(
        weight, tokens_ref[...], (((1,), (1,)), ((), ())), preferred_element_type=F32
    )
    logits = logits.reshape(HEADS, LANES, count)
    logits = jnp.where(iota(logits.shape, 1) < TAPS, logits, -3e38)
    top = jnp.max(logits, axis=1, keepdims=True)
    powers = jnp.exp(logits - top)
    probs = powers / jnp.sum(powers, axis=1, keepdims=True)
    probs_ref[...] = probs.reshape(HEADS * LANES, count).T.astype(BF16)

    experts = capacity_ref.shape[1]
    expert = iota((experts, count), 0)
    onehot = jnp.where(ids_ref[...] == expert, 1.0, 0.0)
    chosen = onehot.astype(BF16)
    later = jnp.where(iota((count, count), 0) < iota((count, count), 1), 1.0, 0.0).astype(BF16)
    before = jnp.dot(chosen, later, preferred_element_type=F32)
    rank = jnp.sum(onehot * before, axis=0, keepdims=True)
    limit = jnp.dot(capacity_ref[...].astype(F32).astype(BF16), chosen, preferred_element_type=F32)
    apart = expert ^ place_ref[0]
    first = ((apart >> 1) + (apart & 1) * (experts // 2)) * depth
    slot = jnp.sum(onehot * first.astype(F32), axis=0, keepdims=True) + rank
    slot = jnp.where(rank < limit, slot, -1.0)
    slot_row_ref[...] = slot.astype(jnp.int32)
    slot_ref[...] = jnp.broadcast_to(slot, (8, count)).T.astype(jnp.int32)
    onehot_ref[...] = onehot.T


def mix_kernel(
    place_ref,
    tokens_ref,
    near_ref,
    cross_ref,
    probs_ref,
    onehot_ref,
    slot_row_ref,
    gain_ref,
    router_ref,
    mixed_ref,
    packed_ref,
    gate_ref,
    padded_ref,
    normed_ref,
):
    count, width = tokens_ref.shape
    padded_ref[pl.ds(0, FRONT), :] = jnp.zeros((FRONT, width), BF16)
    low_core = place_ref[0] % 2 == 0
    near, cross = near_ref[...], cross_ref[...]
    padded_ref[pl.ds(FRONT, HALO), :] = jnp.where(low_core, cross, near)
    padded_ref[pl.ds(FRONT + HALO, count), :] = tokens_ref[...]
    padded_ref[pl.ds(FRONT + HALO + count, HALO), :] = jnp.where(low_core, near, cross)
    after = FRONT + 2 * HALO + count
    padded_ref[pl.ds(after, padded_ref.shape[0] - after), :] = jnp.zeros(
        (padded_ref.shape[0] - after, width), BF16
    )
    offset = iota((BLOCK, 2 * BLOCK), 1) - iota((BLOCK, 2 * BLOCK), 0) - 1
    squares = []
    for block in range(count // BLOCK):
        rows = pl.ds(block * BLOCK, BLOCK)
        square = jnp.zeros((BLOCK, 128), F32)
        for group in range(HEADS // 4):
            taps = probs_ref[rows, pl.ds(group * 128, 128)].astype(F32)
            taps = jnp.concatenate([taps, jnp.zeros((BLOCK, BLOCK), F32)], axis=1)
            band = pltpu.roll(taps, 1, 1, stride=1, stride_axis=0)
            for pair in range(2):
                lanes = pl.ds((group * 2 + pair) * 128, 128)
                halves = []
                for head in (2 * pair, 2 * pair + 1):
                    mine = (offset >= head * LANES) & (offset < (head + 1) * LANES)
                    own = jnp.where(mine, band, 0.0).astype(BF16)
                    start = FRONT + block * BLOCK - LANES * head
                    halves.append(
                        jnp.dot(
                            own,
                            padded_ref[pl.ds(start, 2 * BLOCK), lanes],
                            preferred_element_type=F32,
                        )
                    )
                left = iota((BLOCK, 128), 1) < 64
                mixed = tokens_ref[rows, lanes].astype(F32) + jnp.where(left, halves[0], halves[1])
                mixed_ref[rows, lanes] = mixed
                square = square + mixed * mixed
        squares.append(square)
    gain = gain_ref[...].astype(F32).reshape(1, width)
    for block in range(count // BLOCK):
        rows = pl.ds(block * BLOCK, BLOCK)
        mean = jnp.sum(squares[block], axis=1, keepdims=True) / width
        scale = lax.rsqrt(mean + EPS)
        normed_ref[rows, :] = (mixed_ref[rows, :] * scale * gain).astype(BF16)

    normed = normed_ref[...]
    slots = packed_ref.shape[0] * packed_ref.shape[1] * packed_ref.shape[2]
    select = jnp.where(iota((slots, count), 0) == slot_row_ref[...], 1.0, 0.0).astype(BF16)
    packed = jnp.dot(select, normed, preferred_element_type=F32).astype(BF16)
    packed_ref[...] = packed.reshape(packed_ref.shape)
    gates = lax.dot_general(
        normed, router_ref[...], (((1,), (1,)), ((), ())), preferred_element_type=F32
    )
    gate_ref[...] = jax.nn.sigmoid(jnp.sum(gates * onehot_ref[...], axis=1, keepdims=True))


def combine_kernel(mixed_ref, gate_ref, slot_ref, returned_ref, handed_ref, out_ref):
    count = mixed_ref.shape[0]
    half = returned_ref.shape[0]
    slot = slot_ref[:, :1]
    near = jnp.where(slot == iota((count, half), 1), 1.0, 0.0).astype(BF16)
    cross = jnp.where(slot == iota((count, half), 1) + half, 1.0, 0.0).astype(BF16)
    out = jnp.dot(near, returned_ref[...], preferred_element_type=F32)
    out = out + jnp.dot(cross, handed_ref[...], preferred_element_type=F32)
    out_ref[...] = (mixed_ref[...] + gate_ref[...] * out).astype(BF16)


def act_kernel(pieces, groups, *refs):
    rows_refs, weights = refs[: 2 * groups], refs[2 * groups : 2 * groups + 2 * pieces]
    acts, rows_ref = refs[2 * groups + 2 * pieces : -1], refs[-1]
    size = rows_refs[0].shape[0]
    for index, ref in enumerate(rows_refs):
        rows_ref[pl.ds(index * size, size), :] = ref[...]
    rows = rows_ref[...]
    for piece in range(pieces):
        gate_ref, up_ref = weights[2 * piece : 2 * piece + 2]
        gated = jnp.dot(rows, gate_ref[...], preferred_element_type=F32)
        lifted = jnp.dot(rows, up_ref[...], preferred_element_type=F32)
        acts[piece][...] = (gated / (1.0 + jnp.exp(-gated)) * lifted).astype(BF16)


def down_kernel(pieces, *refs):
    acts, downs, (own_ref, far_ref) = refs[:pieces], refs[pieces : 3 * pieces], refs[3 * pieces :]
    size, width = own_ref.shape
    for half in range(2):
        columns = pl.ds(half * (width // 2), width // 2)
        total = None
        for act_ref, down_ref in zip(acts, downs[half::2], strict=True):
            part = lax.dot_general(
                act_ref[...], down_ref[...], (((1,), (1,)), ((), ())), preferred_element_type=F32
            )
            total = part if total is None else total + part
        own_ref[:, columns] = total[:size]
        far_ref[:, columns] = total[size:].astype(BF16)


def add_kernel(own_ref, other_ref, out_ref):
    out_ref[...] = (own_ref[...] + other_ref[...].astype(F32)).astype(BF16)


def split_kernel(back_ref, returned_ref, handed_ref):
    half = returned_ref.shape[0]
    returned_ref[...] = back_ref[pl.ds(0, half), :]
    handed_ref[...] = back_ref[pl.ds(half, half), :]


def call(kernel, out_shape, scratch=(), in_specs=None):
    extra = {} if in_specs is None else {"in_specs": in_specs}
    return pl.pallas_call(
        kernel,
        out_shape=out_shape,
        scratch_shapes=scratch,
        **extra,
        compiler_params=pltpu.CompilerParams(vmem_limit_bytes=24 * 1024 * 1024),
        cost_estimate=pl.CostEstimate(flops=0, bytes_accessed=0, transcendentals=0),
    )


def shape(dims, dtype):
    return jax.ShapeDtypeStruct(dims, dtype)


def on_device(
    tokens,
    expert_ids,
    expert_capacity,
    kernel_weight,
    norm_gain,
    router,
    expert_gate,
    expert_up,
    expert_down,
):
    local = tokens[0]
    count, width = local.shape
    experts = expert_capacity.shape[0]
    depth = max(2, 2 * count // experts)
    splits = lax.axis_size("blk")
    blocks = lax.axis_size("seq")
    pieces = splits // 2
    chips = blocks // 2

    def across(array, masks):
        pairs = [
            (split * blocks + block, (split ^ masks[block % 2]) * blocks + block)
            for split in range(splits)
            for block in range(blocks)
        ]
        return lax.ppermute(array, ("blk", "seq"), pairs)

    def after(array, earlier):
        return lax.optimization_barrier((array, earlier))[0]

    row_masks = (1, 2)
    weight_masks = [
        [mask for mask in range(1, splits) if not mask & row_mask] for row_mask in row_masks
    ]

    def to_chip(array, apart):
        return lax.ppermute(array, "seq", [(i, i ^ (2 * apart)) for i in range(blocks)])

    def to_core(array):
        return lax.ppermute(array, "seq", [(i, i ^ 1) for i in range(blocks)])

    place = lax.axis_index("seq").astype(jnp.int32).reshape(1)
    sources = [
        local,
        kernel_weight.T,
        expert_ids[0].reshape(1, count),
        expert_capacity[None, :],
        norm_gain,
        router.T,
        expert_down[0],
    ]
    half = (width // 2, expert_down.shape[2])
    hidden = expert_gate.shape[2]
    local, kernel_rows, ids, capacity, gain, columns, *down, near_edge, cross_edge = call(
        fetch_kernel,
        [pltpu.VMEM(array.shape, array.dtype) for array in sources[:-1]]
        + [pltpu.VMEM(half, BF16)] * 2
        + [pltpu.VMEM((HALO, width), BF16)] * 2,
        scratch=(pltpu.SemaphoreType.DMA((len(sources) + 1,)),),
        in_specs=[SMEM] + [HBM] * len(sources),
    )(place, *[pltpu.with_memory_space_constraint(array, pltpu.HBM) for array in sources])
    inner, downs = [expert_gate[0], expert_up[0]], list(down)
    for masks in zip(*weight_masks, strict=True):
        inner += [across(array, masks) for array in inner[:2]]
        downs += [across(after(array, inner[-2]), masks) for array in down]
    near_edge = to_core(near_edge)
    between = [(i, i + 1) for i in range(1, blocks - 1, 2)]
    between += [(target, source) for source, target in between]
    cross_edge = lax.ppermute(cross_edge, "seq", between)
    probs, onehot, slot, slot_row = call(
        functools.partial(probs_kernel, depth),
        (
            shape((count, HEADS * LANES), BF16),
            shape((count, experts), F32),
            shape((count, 8), jnp.int32),
            shape((1, count), jnp.int32),
        ),
        in_specs=[VMEM, VMEM, VMEM, VMEM, SMEM],
    )(local, kernel_rows, ids, capacity, place)
    mixed, packed, gate = call(
        mix_kernel,
        (
            shape((count, width), F32),
            shape((2, chips, depth, width), BF16),
            shape((count, 1), F32),
        ),
        scratch=(
            pltpu.VMEM((FRONT + count + BLOCK, width), BF16),
            pltpu.VMEM((count, width), BF16),
        ),
        in_specs=[SMEM] + [VMEM] * 8,
    )(place, local, near_edge, cross_edge, probs, onehot, slot_row, gain, columns)
    crossed = to_core(packed[1])
    both = jnp.concatenate([packed[0], crossed], axis=1)
    size = 2 * depth
    near = list(range(chips // 2))
    order = [apart for apart in reversed(range(chips)) if apart not in near]
    rows, sums = [None] * chips, [None] * chips

    def arrive(apart, earlier):
        array = both[apart] if earlier is None else after(both[apart], earlier)
        rows[apart] = to_chip(array, apart) if apart else array

    def work(apart, earlier, behind=None):
        if earlier is not None:
            rows[apart] = after(rows[apart], earlier)
        far = across(rows[apart], row_masks)
        own = rows[apart] if behind is None else after(rows[apart], behind)
        acts = call(
            functools.partial(act_kernel, pieces, 1),
            [shape((2 * size, hidden), BF16)] * pieces,
            scratch=(pltpu.VMEM((2 * size, width), BF16),),
        )(own, far, *inner)
        sums[apart] = call(
            functools.partial(down_kernel, pieces),
            (shape((size, width), F32), shape((size, width), BF16)),
        )(*acts, *downs)

    returned, handed = [None] * chips, [None] * chips

    def finish(apart, earlier=None):
        own, other = sums[apart]
        done = call(add_kernel, shape((size, width), BF16))(own, across(other, row_masks))
        sent = done if earlier is None else after(done, earlier)
        back = to_chip(sent, apart) if apart else sent
        returned[apart], handed[apart] = call(
            split_kernel, [shape((depth, width), BF16)] * 2
        )(back)
        return done

    for index, apart in enumerate(order):
        arrive(apart, rows[order[index - 1]] if index else None)
        if index == 0:
            work(apart, tuple(inner[3::2]))
            first = finish(apart)
        else:
            work(apart, sums[order[index - 1]][1], first)
            finish(apart, returned[order[index - 1]])
    for apart in near:
        arrive(apart, None)
        work(apart, sums[order[0]][1])
        finish(apart)
    returned = jnp.concatenate(returned)
    handed = to_core(jnp.concatenate(handed))
    result = call(combine_kernel, shape((count, width), BF16))(mixed, gate, slot, returned, handed)
    return result[None]


def solution(mesh):
    placed = (
        P("blk", "seq", None),
        P("blk", "seq", None),
        P(),
        P(),
        P(),
        P(),
        P("seq", None, "blk"),
        P("seq", None, "blk"),
        P("seq", None, "blk"),
    )
    return jax.shard_map(
        on_device, mesh=mesh, in_specs=placed, out_specs=P("blk", "seq", None), check_vma=False
    )
```

```python
import functools

import jax
import jax.numpy as jnp
from jax import lax
from jax.experimental import pallas as pl
from jax.experimental.pallas import tpu as pltpu
from jax.sharding import PartitionSpec as P

HEADS = 16
TAPS = 31
LANES = 32
HALO = 16
FRONT = 96
BLOCK = 128
EPS = 1e-06

VMEM = pl.BlockSpec(memory_space=pltpu.VMEM)
HBM = pl.BlockSpec(memory_space=pltpu.HBM)
SMEM = pl.BlockSpec(memory_space=pltpu.SMEM)
F32 = jnp.float32
BF16 = jnp.bfloat16


def iota(shape, dim):
    return lax.broadcasted_iota(jnp.int32, shape, dim)


def fetch_kernel(place_ref, *refs):
    count = len(refs) // 2 - 2
    sources, targets, (near_ref, cross_ref, sems) = refs[:count], refs[count:-3], refs[-3:]
    half = sources[-1].shape[0] // 2
    sources = [*sources[:-1], *[sources[-1].at[pl.ds(first, half), :] for first in (0, half)]]
    copies = [
        pltpu.make_async_copy(source, target, sems.at[index])
        for index, (source, target) in enumerate(zip(sources, targets, strict=True))
    ]
    for copy in copies:
        copy.start()
    copies[0].wait()
    tokens_ref = targets[0]
    head = tokens_ref[pl.ds(0, HALO), :]
    tail = tokens_ref[pl.ds(tokens_ref.shape[0] - HALO, HALO), :]
    low_core = place_ref[0] % 2 == 0
    near_ref[...] = jnp.where(low_core, tail, head)
    cross_ref[...] = jnp.where(low_core, head, tail)
    for copy in copies[1:]:
        copy.wait()


def probs_kernel(
    depth,
    tokens_ref,
    weight_ref,
    ids_ref,
    capacity_ref,
    place_ref,
    probs_ref,
    onehot_ref,
    slot_ref,
    slot_row_ref,
):
    count = tokens_ref.shape[0]
    columns = weight_ref.shape[0]
    row = iota((HEADS * LANES, columns), 0)
    column = iota((HEADS * LANES, columns), 1)
    tap = row % LANES
    spread = jnp.where((row // LANES * TAPS + tap == column) & (tap < TAPS), 1.0, 0.0).astype(BF16)
    weight = jnp.dot(spread, weight_ref[...], preferred_element_type=F32).astype(BF16)
    logits = lax.dot_general(
        weight, tokens_ref[...], (((1,), (1,)), ((), ())), preferred_element_type=F32
    )
    logits = logits.reshape(HEADS, LANES, count)
    logits = jnp.where(iota(logits.shape, 1) < TAPS, logits, -3e38)
    top = jnp.max(logits, axis=1, keepdims=True)
    powers = jnp.exp(logits - top)
    probs = powers / jnp.sum(powers, axis=1, keepdims=True)
    probs_ref[...] = probs.reshape(HEADS * LANES, count).T.astype(BF16)

    experts = capacity_ref.shape[1]
    expert = iota((experts, count), 0)
    onehot = jnp.where(ids_ref[...] == expert, 1.0, 0.0)
    chosen = onehot.astype(BF16)
    later = jnp.where(iota((count, count), 0) < iota((count, count), 1), 1.0, 0.0).astype(BF16)
    before = jnp.dot(chosen, later, preferred_element_type=F32)
    rank = jnp.sum(onehot * before, axis=0, keepdims=True)
    limit = jnp.dot(capacity_ref[...].astype(F32).astype(BF16), chosen, preferred_element_type=F32)
    apart = expert ^ place_ref[0]
    first = ((apart >> 1) + (apart & 1) * (experts // 2)) * depth
    slot = jnp.sum(onehot * first.astype(F32), axis=0, keepdims=True) + rank
    slot = jnp.where(rank < limit, slot, -1.0)
    slot_row_ref[...] = slot.astype(jnp.int32)
    slot_ref[...] = jnp.broadcast_to(slot, (8, count)).T.astype(jnp.int32)
    onehot_ref[...] = onehot.T


def mix_kernel(
    place_ref,
    tokens_ref,
    near_ref,
    cross_ref,
    probs_ref,
    onehot_ref,
    slot_row_ref,
    gain_ref,
    router_ref,
    mixed_ref,
    packed_ref,
    gate_ref,
    padded_ref,
    normed_ref,
):
    count, width = tokens_ref.shape
    padded_ref[pl.ds(0, FRONT), :] = jnp.zeros((FRONT, width), BF16)
    low_core = place_ref[0] % 2 == 0
    near, cross = near_ref[...], cross_ref[...]
    padded_ref[pl.ds(FRONT, HALO), :] = jnp.where(low_core, cross, near)
    padded_ref[pl.ds(FRONT + HALO, count), :] = tokens_ref[...]
    padded_ref[pl.ds(FRONT + HALO + count, HALO), :] = jnp.where(low_core, near, cross)
    after = FRONT + 2 * HALO + count
    padded_ref[pl.ds(after, padded_ref.shape[0] - after), :] = jnp.zeros(
        (padded_ref.shape[0] - after, width), BF16
    )
    offset = iota((BLOCK, 2 * BLOCK), 1) - iota((BLOCK, 2 * BLOCK), 0) - 1
    squares = []
    for block in range(count // BLOCK):
        rows = pl.ds(block * BLOCK, BLOCK)
        square = jnp.zeros((BLOCK, 128), F32)
        for group in range(HEADS // 4):
            taps = probs_ref[rows, pl.ds(group * 128, 128)].astype(F32)
            taps = jnp.concatenate([taps, jnp.zeros((BLOCK, BLOCK), F32)], axis=1)
            band = pltpu.roll(taps, 1, 1, stride=1, stride_axis=0)
            for pair in range(2):
                lanes = pl.ds((group * 2 + pair) * 128, 128)
                halves = []
                for head in (2 * pair, 2 * pair + 1):
                    mine = (offset >= head * LANES) & (offset < (head + 1) * LANES)
                    own = jnp.where(mine, band, 0.0).astype(BF16)
                    start = FRONT + block * BLOCK - LANES * head
                    halves.append(
                        jnp.dot(
                            own,
                            padded_ref[pl.ds(start, 2 * BLOCK), lanes],
                            preferred_element_type=F32,
                        )
                    )
                left = iota((BLOCK, 128), 1) < 64
                mixed = tokens_ref[rows, lanes].astype(F32) + jnp.where(left, halves[0], halves[1])
                mixed_ref[rows, lanes] = mixed
                square = square + mixed * mixed
        squares.append(square)
    gain = gain_ref[...].astype(F32).reshape(1, width)
    for block in range(count // BLOCK):
        rows = pl.ds(block * BLOCK, BLOCK)
        mean = jnp.sum(squares[block], axis=1, keepdims=True) / width
        scale = lax.rsqrt(mean + EPS)
        normed_ref[rows, :] = (mixed_ref[rows, :] * scale * gain).astype(BF16)

    normed = normed_ref[...]
    slots = packed_ref.shape[0] * packed_ref.shape[1] * packed_ref.shape[2]
    select = jnp.where(iota((slots, count), 0) == slot_row_ref[...], 1.0, 0.0).astype(BF16)
    packed = jnp.dot(select, normed, preferred_element_type=F32).astype(BF16)
    packed_ref[...] = packed.reshape(packed_ref.shape)
    gates = lax.dot_general(
        normed, router_ref[...], (((1,), (1,)), ((), ())), preferred_element_type=F32
    )
    gate_ref[...] = jax.nn.sigmoid(jnp.sum(gates * onehot_ref[...], axis=1, keepdims=True))


def combine_kernel(places, total_ref, gate_ref, slot_ref, *refs):
    pieces, (out_ref, held_ref) = refs[:-2], refs[-2:]
    count = total_ref.shape[0]
    held = held_ref.shape[0]
    depth = held // len(places)
    first = 0
    for piece_ref in pieces:
        held_ref[pl.ds(first, piece_ref.shape[0]), :] = piece_ref[...]
        first += piece_ref.shape[0]
    place = iota((count, held), 1)
    row = place % depth
    for index, group in enumerate(places):
        row = row + jnp.where(place // depth == index, group * depth, 0)
    select = jnp.where(slot_ref[:, :1] == row, 1.0, 0.0).astype(BF16)
    out = jnp.dot(select, held_ref[...], preferred_element_type=F32)
    out_ref[...] = (total_ref[...] + gate_ref[...] * out).astype(out_ref.dtype)


def act_kernel(pieces, groups, *refs):
    rows_refs, weights = refs[: 2 * groups], refs[2 * groups : 2 * groups + 2 * pieces]
    acts, rows_ref = refs[2 * groups + 2 * pieces : -1], refs[-1]
    size = rows_refs[0].shape[0]
    for index, ref in enumerate(rows_refs):
        rows_ref[pl.ds(index * size, size), :] = ref[...]
    rows = rows_ref[...]
    for piece in range(pieces):
        gate_ref, up_ref = weights[2 * piece : 2 * piece + 2]
        gated = jnp.dot(rows, gate_ref[...], preferred_element_type=F32)
        lifted = jnp.dot(rows, up_ref[...], preferred_element_type=F32)
        acts[piece][...] = (gated / (1.0 + jnp.exp(-gated)) * lifted).astype(BF16)


def down_kernel(pieces, *refs):
    acts, downs, (own_ref, far_ref) = refs[:pieces], refs[pieces : 3 * pieces], refs[3 * pieces :]
    size, width = own_ref.shape
    for half in range(2):
        columns = pl.ds(half * (width // 2), width // 2)
        total = None
        for act_ref, down_ref in zip(acts, downs[half::2], strict=True):
            part = lax.dot_general(
                act_ref[...], down_ref[...], (((1,), (1,)), ((), ())), preferred_element_type=F32
            )
            total = part if total is None else total + part
        own_ref[:, columns] = total[:size]
        far_ref[:, columns] = total[size:].astype(BF16)


def early_kernel(pieces, *refs):
    acts, own_downs, first_halves, total_ref = (
        refs[:pieces],
        refs[pieces : pieces + 2],
        refs[pieces + 2 : -1],
        refs[-1],
    )
    width = total_ref.shape[1]
    for half in range(2):
        downs = [own_downs[half], *(first_halves if half == 0 else ())]
        total = None
        for act_ref, down_ref in zip(acts, downs, strict=False):
            part = lax.dot_general(
                act_ref[...], down_ref[...], (((1,), (1,)), ((), ())), preferred_element_type=F32
            )
            total = part if total is None else total + part
        total_ref[:, pl.ds(half * (width // 2), width // 2)] = total


def late_kernel(pieces, *refs):
    total_ref, acts, downs, (own_ref, far_ref) = refs[0], refs[1:pieces], refs[pieces : 2 * pieces - 1], refs[-2:]
    size, width = own_ref.shape
    first, second = pl.ds(0, width // 2), pl.ds(width // 2, width // 2)
    total = total_ref[:, second]
    for act_ref, down_ref in zip(acts, downs, strict=True):
        total = total + lax.dot_general(
            act_ref[...], down_ref[...], (((1,), (1,)), ((), ())), preferred_element_type=F32
        )
    far_ref[:, first] = total_ref[pl.ds(size, size), first].astype(BF16)
    far_ref[:, second] = total[size:].astype(BF16)
    own_ref[:, first] = total_ref[pl.ds(0, size), first]
    own_ref[:, second] = total[:size]


def add_kernel(own_ref, other_ref, out_ref):
    out_ref[...] = (own_ref[...] + other_ref[...].astype(F32)).astype(BF16)


def split_kernel(back_ref, returned_ref, handed_ref):
    half = returned_ref.shape[0]
    returned_ref[...] = back_ref[pl.ds(0, half), :]
    handed_ref[...] = back_ref[pl.ds(half, half), :]


def call(kernel, out_shape, scratch=(), in_specs=None):
    extra = {} if in_specs is None else {"in_specs": in_specs}
    return pl.pallas_call(
        kernel,
        out_shape=out_shape,
        scratch_shapes=scratch,
        **extra,
        compiler_params=pltpu.CompilerParams(vmem_limit_bytes=24 * 1024 * 1024),
        cost_estimate=pl.CostEstimate(flops=0, bytes_accessed=0, transcendentals=0),
    )


def shape(dims, dtype):
    return jax.ShapeDtypeStruct(dims, dtype)


def on_device(
    tokens,
    expert_ids,
    expert_capacity,
    kernel_weight,
    norm_gain,
    router,
    expert_gate,
    expert_up,
    expert_down,
):
    local = tokens[0]
    count, width = local.shape
    experts = expert_capacity.shape[0]
    depth = max(2, 2 * count // experts)
    splits = lax.axis_size("blk")
    blocks = lax.axis_size("seq")
    pieces = splits // 2
    chips = blocks // 2

    def across(array, masks):
        pairs = [
            (split * blocks + block, (split ^ masks[block % 2]) * blocks + block)
            for split in range(splits)
            for block in range(blocks)
        ]
        return lax.ppermute(array, ("blk", "seq"), pairs)

    def after(array, earlier):
        return lax.optimization_barrier((array, earlier))[0]

    row_masks = (1, 2)
    weight_masks = [
        [mask for mask in range(1, splits) if not mask & row_mask] for row_mask in row_masks
    ]

    def to_chip(array, apart):
        return lax.ppermute(array, "seq", [(i, i ^ (2 * apart)) for i in range(blocks)])

    def to_core(array):
        return lax.ppermute(array, "seq", [(i, i ^ 1) for i in range(blocks)])

    place = lax.axis_index("seq").astype(jnp.int32).reshape(1)
    sources = [
        local,
        kernel_weight.T,
        expert_ids[0].reshape(1, count),
        expert_capacity[None, :],
        norm_gain,
        router.T,
        expert_down[0],
    ]
    half = (width // 2, expert_down.shape[2])
    hidden = expert_gate.shape[2]
    local, kernel_rows, ids, capacity, gain, columns, *down, near_edge, cross_edge = call(
        fetch_kernel,
        [pltpu.VMEM(array.shape, array.dtype) for array in sources[:-1]]
        + [pltpu.VMEM(half, BF16)] * 2
        + [pltpu.VMEM((HALO, width), BF16)] * 2,
        scratch=(pltpu.SemaphoreType.DMA((len(sources) + 1,)),),
        in_specs=[SMEM] + [HBM] * len(sources),
    )(place, *[pltpu.with_memory_space_constraint(array, pltpu.HBM) for array in sources])
    inner, downs = [expert_gate[0], expert_up[0]], list(down)
    for masks in zip(*weight_masks, strict=True):
        inner += [across(array, masks) for array in inner[:2]]
        downs += [across(after(array, inner[-2]), masks) for array in down]
    near_edge = to_core(near_edge)
    between = [(i, i + 1) for i in range(1, blocks - 1, 2)]
    between += [(target, source) for source, target in between]
    cross_edge = lax.ppermute(cross_edge, "seq", between)
    probs, onehot, slot, slot_row = call(
        functools.partial(probs_kernel, depth),
        (
            shape((count, HEADS * LANES), BF16),
            shape((count, experts), F32),
            shape((count, 8), jnp.int32),
            shape((1, count), jnp.int32),
        ),
        in_specs=[VMEM, VMEM, VMEM, VMEM, SMEM],
    )(local, kernel_rows, ids, capacity, place)
    mixed, packed, gate = call(
        mix_kernel,
        (
            shape((count, width), F32),
            shape((2, chips, depth, width), BF16),
            shape((count, 1), F32),
        ),
        scratch=(
            pltpu.VMEM((FRONT + count + BLOCK, width), BF16),
            pltpu.VMEM((count, width), BF16),
        ),
        in_specs=[SMEM] + [VMEM] * 8,
    )(place, local, near_edge, cross_edge, probs, onehot, slot_row, gain, columns)
    crossed = to_core(packed[1])
    both = jnp.concatenate([packed[0], crossed], axis=1)
    size = 2 * depth
    near = list(range(chips // 2))
    order = [apart for apart in reversed(range(chips)) if apart not in near]
    rows, sums = [None] * chips, [None] * chips

    def arrive(apart, earlier):
        array = both[apart] if earlier is None else after(both[apart], earlier)
        rows[apart] = to_chip(array, apart) if apart else array

    def work(apart, earlier, behind=None):
        if earlier is not None:
            rows[apart] = after(rows[apart], earlier)
        far = across(rows[apart], row_masks)
        own = rows[apart] if behind is None else after(rows[apart], behind)
        acts = call(
            functools.partial(act_kernel, pieces, 1),
            [shape((2 * size, hidden), BF16)] * pieces,
            scratch=(pltpu.VMEM((2 * size, width), BF16),),
        )(own, far, *inner)
        sums[apart] = call(
            functools.partial(down_kernel, pieces),
            (shape((size, width), F32), shape((size, width), BF16)),
        )(*acts, *downs)

    returned, handed = [None] * chips, [None] * chips

    def finish(apart, earlier=None):
        own, other = sums[apart]
        done = call(add_kernel, shape((size, width), BF16))(own, across(other, row_masks))
        sent = done if earlier is None else after(done, earlier)
        back = to_chip(sent, apart) if apart else sent
        returned[apart], handed[apart] = call(
            split_kernel, [shape((depth, width), BF16)] * 2
        )(back)
        return done

    for index, apart in enumerate(order):
        arrive(apart, rows[order[index - 1]] if index else None)
        if index == 0:
            work(apart, tuple(inner[3::2]))
            first = finish(apart)
        else:
            work(apart, sums[order[index - 1]][1], first)
            finish(apart, returned[order[index - 1]])
    for apart in near:
        arrive(apart, None)
        work(apart, sums[order[0]][1])
        finish(apart)
    def combine(total, places, arrays, dtype):
        return call(
            functools.partial(combine_kernel, tuple(places)),
            shape((count, width), dtype),
            scratch=(pltpu.VMEM((len(places) * depth, width), BF16),),
        )(total, gate, slot, *arrays)

    late = [apart for apart in range(chips) if apart in order[1:] or apart == near[-1]]
    early = [apart for apart in range(chips) if apart not in late]
    soon = to_core(jnp.concatenate([handed[apart] for apart in early]))
    last = to_core(jnp.concatenate([handed[apart] for apart in late]))
    places = list(range(chips)) + [chips + apart for apart in early]
    total = combine(mixed, places, [*returned, soon], F32)
    return combine(total, [chips + apart for apart in late], [last], BF16)[None]


def solution(mesh):
    placed = (
        P("blk", "seq", None),
        P("blk", "seq", None),
        P(),
        P(),
        P(),
        P(),
        P("seq", None, "blk"),
        P("seq", None, "blk"),
        P("seq", None, "blk"),
    )
    return jax.shard_map(
        on_device, mesh=mesh, in_specs=placed, out_specs=P("blk", "seq", None), check_vma=False
    )
```

```python
import functools

import jax
import jax.numpy as jnp
from jax import lax
from jax.experimental import pallas as pl
from jax.experimental.pallas import tpu as pltpu
from jax.sharding import PartitionSpec as P

HEADS = 16
TAPS = 31
LANES = 32
HALO = 16
FRONT = 96
BLOCK = 128
EPS = 1e-06

VMEM = pl.BlockSpec(memory_space=pltpu.VMEM)
HBM = pl.BlockSpec(memory_space=pltpu.HBM)
SMEM = pl.BlockSpec(memory_space=pltpu.SMEM)
F32 = jnp.float32
BF16 = jnp.bfloat16


def iota(shape, dim):
    return lax.broadcasted_iota(jnp.int32, shape, dim)


def fetch_kernel(place_ref, *refs):
    count = len(refs) // 2 - 2
    sources, targets, (near_ref, cross_ref, sems) = refs[:count], refs[count:-3], refs[-3:]
    half = sources[-1].shape[0] // 2
    sources = [*sources[:-1], *[sources[-1].at[pl.ds(first, half), :] for first in (0, half)]]
    copies = [
        pltpu.make_async_copy(source, target, sems.at[index])
        for index, (source, target) in enumerate(zip(sources, targets, strict=True))
    ]
    for copy in copies:
        copy.start()
    copies[0].wait()
    tokens_ref = targets[0]
    head = tokens_ref[pl.ds(0, HALO), :]
    tail = tokens_ref[pl.ds(tokens_ref.shape[0] - HALO, HALO), :]
    low_core = place_ref[0] % 2 == 0
    near_ref[...] = jnp.where(low_core, tail, head)
    cross_ref[...] = jnp.where(low_core, head, tail)
    for copy in copies[1:]:
        copy.wait()


def probs_kernel(
    depth,
    tokens_ref,
    weight_ref,
    ids_ref,
    capacity_ref,
    place_ref,
    probs_ref,
    onehot_ref,
    slot_ref,
    slot_row_ref,
):
    count = tokens_ref.shape[0]
    columns = weight_ref.shape[0]
    row = iota((HEADS * LANES, columns), 0)
    column = iota((HEADS * LANES, columns), 1)
    tap = row % LANES
    spread = jnp.where((row // LANES * TAPS + tap == column) & (tap < TAPS), 1.0, 0.0).astype(BF16)
    weight = jnp.dot(spread, weight_ref[...], preferred_element_type=F32).astype(BF16)
    logits = lax.dot_general(
        weight, tokens_ref[...], (((1,), (1,)), ((), ())), preferred_element_type=F32
    )
    logits = logits.reshape(HEADS, LANES, count)
    logits = jnp.where(iota(logits.shape, 1) < TAPS, logits, -3e38)
    top = jnp.max(logits, axis=1, keepdims=True)
    powers = jnp.exp(logits - top)
    probs = powers / jnp.sum(powers, axis=1, keepdims=True)
    probs_ref[...] = probs.reshape(HEADS * LANES, count).T.astype(BF16)

    experts = capacity_ref.shape[1]
    expert = iota((experts, count), 0)
    onehot = jnp.where(ids_ref[...] == expert, 1.0, 0.0)
    chosen = onehot.astype(BF16)
    later = jnp.where(iota((count, count), 0) < iota((count, count), 1), 1.0, 0.0).astype(BF16)
    before = jnp.dot(chosen, later, preferred_element_type=F32)
    rank = jnp.sum(onehot * before, axis=0, keepdims=True)
    limit = jnp.dot(capacity_ref[...].astype(F32).astype(BF16), chosen, preferred_element_type=F32)
    apart = expert ^ place_ref[0]
    first = ((apart >> 1) + (apart & 1) * (experts // 2)) * depth
    slot = jnp.sum(onehot * first.astype(F32), axis=0, keepdims=True) + rank
    slot = jnp.where(rank < limit, slot, -1.0)
    slot_row_ref[...] = slot.astype(jnp.int32)
    slot_ref[...] = jnp.broadcast_to(slot, (8, count)).T.astype(jnp.int32)
    onehot_ref[...] = onehot.T


def mix_kernel(
    place_ref,
    tokens_ref,
    near_ref,
    cross_ref,
    probs_ref,
    onehot_ref,
    slot_row_ref,
    gain_ref,
    router_ref,
    mixed_ref,
    packed_ref,
    gate_ref,
    padded_ref,
    normed_ref,
):
    count, width = tokens_ref.shape
    padded_ref[pl.ds(0, FRONT), :] = jnp.zeros((FRONT, width), BF16)
    low_core = place_ref[0] % 2 == 0
    near, cross = near_ref[...], cross_ref[...]
    padded_ref[pl.ds(FRONT, HALO), :] = jnp.where(low_core, cross, near)
    padded_ref[pl.ds(FRONT + HALO, count), :] = tokens_ref[...]
    padded_ref[pl.ds(FRONT + HALO + count, HALO), :] = jnp.where(low_core, near, cross)
    after = FRONT + 2 * HALO + count
    padded_ref[pl.ds(after, padded_ref.shape[0] - after), :] = jnp.zeros(
        (padded_ref.shape[0] - after, width), BF16
    )
    offset = iota((BLOCK, 2 * BLOCK), 1) - iota((BLOCK, 2 * BLOCK), 0) - 1
    squares = []
    for block in range(count // BLOCK):
        rows = pl.ds(block * BLOCK, BLOCK)
        square = jnp.zeros((BLOCK, 128), F32)
        for group in range(HEADS // 4):
            taps = probs_ref[rows, pl.ds(group * 128, 128)].astype(F32)
            taps = jnp.concatenate([taps, jnp.zeros((BLOCK, BLOCK), F32)], axis=1)
            band = pltpu.roll(taps, 1, 1, stride=1, stride_axis=0)
            for pair in range(2):
                lanes = pl.ds((group * 2 + pair) * 128, 128)
                halves = []
                for head in (2 * pair, 2 * pair + 1):
                    mine = (offset >= head * LANES) & (offset < (head + 1) * LANES)
                    own = jnp.where(mine, band, 0.0).astype(BF16)
                    start = FRONT + block * BLOCK - LANES * head
                    halves.append(
                        jnp.dot(
                            own,
                            padded_ref[pl.ds(start, 2 * BLOCK), lanes],
                            preferred_element_type=F32,
                        )
                    )
                left = iota((BLOCK, 128), 1) < 64
                mixed = tokens_ref[rows, lanes].astype(F32) + jnp.where(left, halves[0], halves[1])
                mixed_ref[rows, lanes] = mixed
                square = square + mixed * mixed
        squares.append(square)
    gain = gain_ref[...].astype(F32).reshape(1, width)
    for block in range(count // BLOCK):
        rows = pl.ds(block * BLOCK, BLOCK)
        mean = jnp.sum(squares[block], axis=1, keepdims=True) / width
        scale = lax.rsqrt(mean + EPS)
        normed_ref[rows, :] = (mixed_ref[rows, :] * scale * gain).astype(BF16)

    normed = normed_ref[...]
    slots = packed_ref.shape[0] * packed_ref.shape[1] * packed_ref.shape[2]
    select = jnp.where(iota((slots, count), 0) == slot_row_ref[...], 1.0, 0.0).astype(BF16)
    packed = jnp.dot(select, normed, preferred_element_type=F32).astype(BF16)
    packed_ref[...] = packed.reshape(packed_ref.shape)
    gates = lax.dot_general(
        normed, router_ref[...], (((1,), (1,)), ((), ())), preferred_element_type=F32
    )
    gate_ref[...] = jax.nn.sigmoid(jnp.sum(gates * onehot_ref[...], axis=1, keepdims=True))


def combine_kernel(places, total_ref, gate_ref, slot_ref, *refs):
    pieces, (out_ref, held_ref) = refs[:-2], refs[-2:]
    count = total_ref.shape[0]
    held = held_ref.shape[0]
    depth = held // len(places)
    first = 0
    for piece_ref in pieces:
        held_ref[pl.ds(first, piece_ref.shape[0]), :] = piece_ref[...]
        first += piece_ref.shape[0]
    place = iota((count, held), 1)
    row = place % depth
    for index, group in enumerate(places):
        row = row + jnp.where(place // depth == index, group * depth, 0)
    select = jnp.where(slot_ref[:, :1] == row, 1.0, 0.0).astype(BF16)
    out = jnp.dot(select, held_ref[...], preferred_element_type=F32)
    out_ref[...] = (total_ref[...] + gate_ref[...] * out).astype(out_ref.dtype)


def act_kernel(pieces, groups, *refs):
    rows_refs, weights = refs[: 2 * groups], refs[2 * groups : 2 * groups + 2 * pieces]
    acts, rows_ref = refs[2 * groups + 2 * pieces : -1], refs[-1]
    size = rows_refs[0].shape[0]
    for index, ref in enumerate(rows_refs):
        rows_ref[pl.ds(index * size, size), :] = ref[...]
    rows = rows_ref[...]
    for piece in range(pieces):
        gate_ref, up_ref = weights[2 * piece : 2 * piece + 2]
        gated = jnp.dot(rows, gate_ref[...], preferred_element_type=F32)
        lifted = jnp.dot(rows, up_ref[...], preferred_element_type=F32)
        acts[piece][...] = (gated / (1.0 + jnp.exp(-gated)) * lifted).astype(BF16)


def down_kernel(pieces, *refs):
    acts, downs, (own_ref, far_ref) = refs[:pieces], refs[pieces : 3 * pieces], refs[3 * pieces :]
    size, width = own_ref.shape
    for half in range(2):
        columns = pl.ds(half * (width // 2), width // 2)
        total = None
        for act_ref, down_ref in zip(acts, downs[half::2], strict=True):
            part = lax.dot_general(
                act_ref[...], down_ref[...], (((1,), (1,)), ((), ())), preferred_element_type=F32
            )
            total = part if total is None else total + part
        own_ref[:, columns] = total[:size]
        far_ref[:, columns] = total[size:].astype(BF16)


def early_kernel(pieces, *refs):
    acts, own_downs, first_halves, total_ref = (
        refs[:pieces],
        refs[pieces : pieces + 2],
        refs[pieces + 2 : -1],
        refs[-1],
    )
    width = total_ref.shape[1]
    for half in range(2):
        downs = [own_downs[half], *(first_halves if half == 0 else ())]
        total = None
        for act_ref, down_ref in zip(acts, downs, strict=False):
            part = lax.dot_general(
                act_ref[...], down_ref[...], (((1,), (1,)), ((), ())), preferred_element_type=F32
            )
            total = part if total is None else total + part
        total_ref[:, pl.ds(half * (width // 2), width // 2)] = total


def late_kernel(pieces, *refs):
    total_ref, acts, downs, (own_ref, far_ref) = refs[0], refs[1:pieces], refs[pieces : 2 * pieces - 1], refs[-2:]
    size, width = own_ref.shape
    first, second = pl.ds(0, width // 2), pl.ds(width // 2, width // 2)
    total = total_ref[:, second]
    for act_ref, down_ref in zip(acts, downs, strict=True):
        total = total + lax.dot_general(
            act_ref[...], down_ref[...], (((1,), (1,)), ((), ())), preferred_element_type=F32
        )
    far_ref[:, first] = total_ref[pl.ds(size, size), first].astype(BF16)
    far_ref[:, second] = total[size:].astype(BF16)
    own_ref[:, first] = total_ref[pl.ds(0, size), first]
    own_ref[:, second] = total[:size]


def add_kernel(own_ref, other_ref, out_ref):
    out_ref[...] = (own_ref[...] + other_ref[...].astype(F32)).astype(BF16)


def split_kernel(back_ref, returned_ref, handed_ref):
    half = returned_ref.shape[0]
    returned_ref[...] = back_ref[pl.ds(0, half), :]
    handed_ref[...] = back_ref[pl.ds(half, half), :]


def call(kernel, out_shape, scratch=(), in_specs=None):
    extra = {} if in_specs is None else {"in_specs": in_specs}
    return pl.pallas_call(
        kernel,
        out_shape=out_shape,
        scratch_shapes=scratch,
        **extra,
        compiler_params=pltpu.CompilerParams(vmem_limit_bytes=24 * 1024 * 1024),
        cost_estimate=pl.CostEstimate(flops=0, bytes_accessed=0, transcendentals=0),
    )


def shape(dims, dtype):
    return jax.ShapeDtypeStruct(dims, dtype)


def on_device(
    tokens,
    expert_ids,
    expert_capacity,
    kernel_weight,
    norm_gain,
    router,
    expert_gate,
    expert_up,
    expert_down,
):
    local = tokens[0]
    count, width = local.shape
    experts = expert_capacity.shape[0]
    depth = max(2, 2 * count // experts)
    splits = lax.axis_size("blk")
    blocks = lax.axis_size("seq")
    pieces = splits // 2
    chips = blocks // 2

    def across(array, masks):
        pairs = [
            (split * blocks + block, (split ^ masks[block % 2]) * blocks + block)
            for split in range(splits)
            for block in range(blocks)
        ]
        return lax.ppermute(array, ("blk", "seq"), pairs)

    def after(array, earlier):
        return lax.optimization_barrier((array, earlier))[0]

    row_masks = (1, 2)
    weight_masks = [
        [mask for mask in range(1, splits) if not mask & row_mask] for row_mask in row_masks
    ]

    def to_chip(array, apart):
        return lax.ppermute(array, "seq", [(i, i ^ (2 * apart)) for i in range(blocks)])

    def to_core(array):
        return lax.ppermute(array, "seq", [(i, i ^ 1) for i in range(blocks)])

    place = lax.axis_index("seq").astype(jnp.int32).reshape(1)
    sources = [
        local,
        kernel_weight.T,
        expert_ids[0].reshape(1, count),
        expert_capacity[None, :],
        expert_down[0],
    ]
    half = (width // 2, expert_down.shape[2])
    hidden = expert_gate.shape[2]
    local, kernel_rows, ids, capacity, *down, near_edge, cross_edge = call(
        fetch_kernel,
        [pltpu.VMEM(array.shape, array.dtype) for array in sources[:-1]]
        + [pltpu.VMEM(half, BF16)] * 2
        + [pltpu.VMEM((HALO, width), BF16)] * 2,
        scratch=(pltpu.SemaphoreType.DMA((len(sources) + 1,)),),
        in_specs=[SMEM] + [HBM] * len(sources),
    )(place, *[pltpu.with_memory_space_constraint(array, pltpu.HBM) for array in sources])
    inner, downs = [expert_gate[0], expert_up[0]], list(down)
    for masks in zip(*weight_masks, strict=True):
        inner += [across(array, masks) for array in inner[:2]]
        downs += [across(after(array, inner[-2]), masks) for array in down]
    near_edge = to_core(near_edge)
    between = [(i, i + 1) for i in range(1, blocks - 1, 2)]
    between += [(target, source) for source, target in between]
    cross_edge = lax.ppermute(cross_edge, "seq", between)
    probs, onehot, slot, slot_row = call(
        functools.partial(probs_kernel, depth),
        (
            shape((count, HEADS * LANES), BF16),
            shape((count, experts), F32),
            shape((count, 8), jnp.int32),
            shape((1, count), jnp.int32),
        ),
        in_specs=[VMEM, VMEM, VMEM, VMEM, SMEM],
    )(local, kernel_rows, ids, capacity, place)
    mixed, packed, gate = call(
        mix_kernel,
        (
            shape((count, width), F32),
            shape((2, chips, depth, width), BF16),
            shape((count, 1), F32),
        ),
        scratch=(
            pltpu.VMEM((FRONT + count + BLOCK, width), BF16),
            pltpu.VMEM((count, width), BF16),
        ),
        in_specs=[SMEM] + [VMEM] * 8,
    )(
        place,
        local,
        near_edge,
        cross_edge,
        probs,
        onehot,
        slot_row,
        norm_gain[None, :],
        router.T,
    )
    crossed = to_core(packed[1])
    both = jnp.concatenate([packed[0], crossed], axis=1)
    size = 2 * depth
    near = list(range(chips // 2))
    order = [apart for apart in reversed(range(chips)) if apart not in near]
    rows, sums = [None] * chips, [None] * chips

    def arrive(apart, earlier):
        array = both[apart] if earlier is None else after(both[apart], earlier)
        rows[apart] = to_chip(array, apart) if apart else array

    def work(apart, earlier, behind=None):
        if earlier is not None:
            rows[apart] = after(rows[apart], earlier)
        far = across(rows[apart], row_masks)
        own = rows[apart] if behind is None else after(rows[apart], behind)
        acts = call(
            functools.partial(act_kernel, pieces, 1),
            [shape((2 * size, hidden), BF16)] * pieces,
            scratch=(pltpu.VMEM((2 * size, width), BF16),),
        )(own, far, *inner)
        sums[apart] = call(
            functools.partial(down_kernel, pieces),
            (shape((size, width), F32), shape((size, width), BF16)),
        )(*acts, *downs)

    returned, handed = [None] * chips, [None] * chips

    def finish(apart, earlier=None):
        own, other = sums[apart]
        done = call(add_kernel, shape((size, width), BF16))(own, across(other, row_masks))
        sent = done if earlier is None else after(done, earlier)
        back = to_chip(sent, apart) if apart else sent
        returned[apart], handed[apart] = call(
            split_kernel, [shape((depth, width), BF16)] * 2
        )(back)
        return done

    for index, apart in enumerate(order):
        arrive(apart, rows[order[index - 1]] if index else None)
        if index == 0:
            work(apart, tuple(inner[3::2]))
            first = finish(apart)
        else:
            work(apart, sums[order[index - 1]][1], first)
            finish(apart, returned[order[index - 1]])
    for apart in near:
        arrive(apart, None)
        work(apart, sums[order[0]][1])
        finish(apart)

    def combine(total, places, arrays, dtype):
        return call(
            functools.partial(combine_kernel, tuple(places)),
            shape((count, width), dtype),
            scratch=(pltpu.VMEM((len(places) * depth, width), BF16),),
        )(total, gate, slot, *arrays)

    late = [apart for apart in range(chips) if apart in order[1:] or apart == near[-1]]
    early = [apart for apart in range(chips) if apart not in late]
    soon = to_core(jnp.concatenate([handed[apart] for apart in early]))
    last = to_core(jnp.concatenate([handed[apart] for apart in late]))
    places = list(range(chips)) + [chips + apart for apart in early]
    total = combine(mixed, places, [*returned, soon], F32)
    return combine(total, [chips + apart for apart in late], [last], BF16)[None]


def solution(mesh):
    placed = (
        P("blk", "seq", None),
        P("blk", "seq", None),
        P(),
        P(),
        P(),
        P(),
        P("seq", None, "blk"),
        P("seq", None, "blk"),
        P("seq", None, "blk"),
    )
    return jax.shard_map(
        on_device, mesh=mesh, in_specs=placed, out_specs=P("blk", "seq", None), check_vma=False
    )
```
